32 devices in a mesh: pool: 2 (over y), inst: 4 (over z), tp: 4 (over x, core).
Axes of the slice: x: 2, y: 2, z: 4, core: 2. Of those that a mesh axis runs over, the one named last changes fastest.
Arguments:
- prefill_q: bfloat16 [8, 768, 8, 1024], P(('pool', 'inst'), None, 'tp'), parts along dimension 0, may hold values from -8 to 8
- prefill_kv: bfloat16 [8, 2, 768, 8, 128], P(('pool', 'inst'), None, None, 'tp'), parts along dimension 0, may hold values from -8 to 8
- span_len: int32 [8], P(('pool', 'inst')), parts along dimension 0, may hold values from 1 to 768, as said below
- page_seg: int32 [8, 24], P(('pool', 'inst')), parts along dimension 0, may hold values from 0 to 12, as said below
- page_dest: int32 [8, 24, 1], P(('pool', 'inst')), parts along dimension 0, may hold values from 0 to 3, as said below
- page_row: int32 [8, 24], P(('pool', 'inst')), parts along dimension 0, may hold values from 0 to 15, as said below
- dec_q: bfloat16 [8, 16, 2, 8, 1024], P(('pool', 'inst'), None, None, 'tp'), parts along dimension 0, may hold values from -8 to 8
- dec_new: bfloat16 [8, 16, 2, 2, 8, 128], P(('pool', 'inst'), None, None, None, 'tp'), parts along dimension 0, may hold values from -6 to 6
- cache_kv: bfloat16 [8, 64, 2, 32, 8, 128], P(('pool', 'inst'), None, None, None, 'tp'), parts along dimension 0, may hold values from -8 to 8
- block_table: int32 [8, 64], P(('pool', 'inst')), parts along dimension 0, may hold values from 0 to 63, each once within a row
- cache_len: int32 [8, 16], P(('pool', 'inst')), parts along dimension 0, may hold values from 2 to 128, as said below
Outputs:
- prefill_out: bfloat16 [8, 768, 8, 1024], P(('pool', 'inst'), None, 'tp'), parts along dimension 0
- dec_out: bfloat16 [8, 16, 2, 8, 1024], P(('pool', 'inst'), None, None, 'tp'), parts along dimension 0
The draws below stay inside these ranges and needn't reach their ends.
There are 2 independent parts, one for each index of `pool`. The reference program is written for one: setup_inputs(seed, part) draws one part's arguments, and reference() takes and returns one part's arrays. A program takes and returns all parts, laid end to end along the dimension named above; each array names one. Nothing has to cross between parts.
Inputs may be any that keep to these rules, and one draw needn't show every extreme that they name: `span_len`: some instance's block is full. `page_seg`: never falls along a block, starts at 0 and rises by one from request to request; each request holds 1 to 12 whole pages, and the first request of every block exactly 12. `page_dest`: all pages of one request go to one decode instance; from one instance at most 12 pages go to one decode instance, and exactly that many in every instance. `page_row`: all pages of one request join one row. `block_table`: each instance's row holds each of its pool pages once. `cache_len`: some row holds 128 tokens.
All inputs are finite; a program needn't handle non-finite values.
Results may differ from the reference program's by a relative error of at most 0.0033.
Values may be sent and summed in bfloat16 or wider, within the bound.
No kernel may reach another device: no remote copies, remote signals or barrier semaphores. Data moves between devices by JAX's collectives and lax.ppermute only.
A program may use at most 128 MiB of HBM per device.

```python
import jax
import jax.numpy as jnp
from jax import lax

HEADS_KV = 8
GROUP = 8
HEAD_DIM = 128
SPAN = 768
ROWS = 16
PAGE = 32
PAGES_MAX = 4
STEPS = 2
INSTANCES = 4
PAGES_SPAN = 24
POOL = 64
CAPACITY = 12


def segment_layout(key):
    layout_key = jax.random.fold_in(key, 31)
    flags = jax.random.bernoulli(layout_key, 0.5, (INSTANCES, PAGES_SPAN))
    last_inst = jnp.arange(INSTANCES, dtype=jnp.int32)[:, None] == INSTANCES - 1
    flags = flags | last_inst
    pages = jnp.arange(PAGES_SPAN, dtype=jnp.int32)[None, :]
    starts = flags | (pages % CAPACITY == 0)
    starts = jnp.where((pages > 0) & (pages < CAPACITY), False, starts)
    segments = jnp.cumsum(starts.astype(jnp.int32), 1) - 1
    return segments.astype(jnp.int32)


def draw_page_seg(key, part):
    segments = segment_layout(key)
    return segments


def draw_page_dest(key, part):
    key = jax.random.fold_in(key, 32)
    orders = jax.vmap(lambda item: jax.random.permutation(item, INSTANCES))(jax.random.split(key, INSTANCES))
    window = jnp.arange(PAGES_SPAN, dtype=jnp.int32) // CAPACITY
    return orders[:, window][:, :, None].astype(jnp.int32)


def draw_page_row(key, part):
    segments = segment_layout(key)
    key = jax.random.fold_in(key, 33)
    picks = jax.random.randint(key, (INSTANCES, PAGES_SPAN), 0, ROWS)
    return jnp.take_along_axis(picks, segments, 1).astype(jnp.int32)


def draw_prefill_q(key, part):
    key = jax.random.fold_in(key, 11)
    shape = (INSTANCES, SPAN, HEADS_KV, GROUP * HEAD_DIM)
    field = jnp.clip(jax.random.normal(key, shape, jnp.float32), -6.0, 6.0)
    return field.astype(jnp.bfloat16)


def draw_prefill_kv(key, part):
    key = jax.random.fold_in(key, 12)
    shape = (INSTANCES, 2, SPAN, HEADS_KV, HEAD_DIM)
    field = jnp.clip(jax.random.normal(key, shape, jnp.float32), -6.0, 6.0)
    return field.astype(jnp.bfloat16)


def draw_dec_q(key, part):
    key = jax.random.fold_in(key, 13)
    shape = (INSTANCES, ROWS, STEPS, HEADS_KV, GROUP * HEAD_DIM)
    field = jnp.clip(jax.random.normal(key, shape, jnp.float32), -6.0, 6.0)
    return field.astype(jnp.bfloat16)


def draw_cache_kv(key, part):
    key = jax.random.fold_in(key, 14)
    shape = (INSTANCES, POOL, 2, PAGE, HEADS_KV, HEAD_DIM)
    field = jnp.clip(jax.random.normal(key, shape, jnp.float32), -6.0, 6.0)
    return field.astype(jnp.bfloat16)


def draw_span_len(key, part):
    key = jax.random.fold_in(key, 21)
    first_key, second_key = jax.random.split(key)
    lengths = jax.random.randint(first_key, (INSTANCES,), 1, SPAN + 1)
    full_index = jax.random.randint(second_key, (), 0, INSTANCES)
    return jnp.where(jnp.arange(INSTANCES) == full_index, SPAN, lengths).astype(jnp.int32)


def draw_cache_len(key, part):
    key = jax.random.fold_in(key, 22)
    first_key, second_key, third_key = jax.random.split(key, 3)
    longest = PAGES_MAX * PAGE
    levels = jax.random.randint(first_key, (INSTANCES, 1), 1, 5)
    limits = levels * longest // 4
    raw = jax.random.randint(second_key, (INSTANCES, ROWS), 0, 65536)
    lengths = 2 + raw % (limits - 1)
    full_index = jax.random.randint(third_key, (), 0, INSTANCES * ROWS)
    flat_ids = jnp.arange(INSTANCES * ROWS).reshape(INSTANCES, ROWS)
    return jnp.where(flat_ids == full_index, longest, lengths).astype(jnp.int32)


def level_of(rng, dims, cuts, low, top_value):
    loudness = 1.0
    for position, shards_of in cuts:
        draws = jax.random.uniform(jax.random.fold_in(jax.random.fold_in(rng, 6), position), (shards_of,), jnp.float32, low / len(cuts), top_value / len(cuts))
        loudness = loudness * jnp.repeat(jnp.exp(draws), dims[position] // shards_of).reshape((-1,) + (1,) * (len(dims) - 1 - position))
    return loudness


def centred(stream_key, shape, spread, reach, cuts=(), held_as=jnp.bfloat16):
    gain = level_of(stream_key, shape, cuts, -0.22, 0.18) if cuts else 1.0
    values = jax.random.normal(stream_key, shape, jnp.float32) * spread * gain
    return jnp.minimum(jnp.maximum(values, -reach), reach).astype(held_as)


def setup_inputs(seed: int = 0, part: int = 0) -> dict:
    key_list = jax.random.split(jax.random.key(seed), 12)
    own_keys = jax.random.split(jax.random.fold_in(key_list[11], part), 12)
    prefill_q = draw_prefill_q(jax.random.fold_in(jax.random.fold_in(key_list[11], part), 71), part)
    prefill_kv = draw_prefill_kv(jax.random.fold_in(jax.random.fold_in(key_list[11], part), 71), part)
    span_len = draw_span_len(jax.random.fold_in(jax.random.fold_in(key_list[11], part), 71), part)
    page_seg = draw_page_seg(jax.random.fold_in(jax.random.fold_in(key_list[11], part), 71), part)
    page_dest = draw_page_dest(jax.random.fold_in(jax.random.fold_in(key_list[11], part), 71), part)
    page_row = draw_page_row(jax.random.fold_in(jax.random.fold_in(key_list[11], part), 71), part)
    dec_q = draw_dec_q(jax.random.fold_in(jax.random.fold_in(key_list[11], part), 71), part)
    dec_new = centred(own_keys[7], (INSTANCES, ROWS, STEPS, 2, HEADS_KV, HEAD_DIM), 1.0, 6.0, ((0, 4), (4, 4)))
    cache_kv = draw_cache_kv(jax.random.fold_in(jax.random.fold_in(key_list[11], part), 71), part)
    block_table = jax.vmap(lambda own: jax.random.permutation(own, POOL))(jax.random.split(own_keys[9], INSTANCES)).reshape((INSTANCES, POOL)).astype(jnp.int32)
    cache_len = draw_cache_len(jax.random.fold_in(jax.random.fold_in(key_list[11], part), 71), part)
    return {"prefill_q": prefill_q, "prefill_kv": prefill_kv, "span_len": span_len, "page_seg": page_seg, "page_dest": page_dest, "page_row": page_row, "dec_q": dec_q, "dec_new": dec_new, "cache_kv": cache_kv, "block_table": block_table, "cache_len": cache_len}


NEGATIVE = -1e30
PRECISE = lax.Precision.HIGHEST


def combine(first, second):
    first_top, first_total, first_acc = first
    second_top, second_total, second_acc = second
    joined = jnp.maximum(first_top, second_top)
    first_factor = jnp.exp(first_top - joined)
    second_factor = jnp.exp(second_top - joined)
    return (joined, first_total * first_factor + second_total * second_factor,
            first_acc * first_factor[..., None] + second_acc * second_factor[..., None])


def prefill_single(queries, keys_vals, length, segments):
    span_size, head_count, row_width = queries.shape
    head_dim = keys_vals.shape[-1]
    scaling = head_dim ** -0.5
    page_size = span_size // segments.shape[0]
    query_f = queries.reshape(span_size, head_count, row_width // head_dim, head_dim).astype(jnp.float32)
    key_f = keys_vals[0].astype(jnp.float32)
    value_f = keys_vals[1].astype(jnp.float32)
    scores = jnp.einsum('qhgd,khd->hgqk', query_f, key_f, precision=PRECISE) * scaling
    positions = jnp.arange(span_size, dtype=jnp.int32)
    token_seg = jnp.repeat(segments, page_size)
    allowed = (positions[None, :] <= positions[:, None]) & (positions[None, :] < length)
    allowed = allowed & (token_seg[None, :] == token_seg[:, None])
    scores = jnp.where(allowed, scores, NEGATIVE)
    row_top = jnp.max(scores, -1, keepdims=True)
    weights_f = jnp.exp(scores - row_top)
    totals = jnp.sum(weights_f, -1)
    rounded = lax.optimization_barrier(weights_f.astype(jnp.bfloat16))
    blended = jnp.einsum('hgqk,khd->qhgd', rounded.astype(jnp.float32), value_f, precision=PRECISE)
    blended = blended / jnp.transpose(totals, (2, 0, 1))[..., None]
    blended = jnp.where((positions < length)[:, None, None, None], blended, 0.0)
    return blended.reshape(span_size, head_count, row_width).astype(jnp.bfloat16)


def cache_partial(query_f, pool, table, lengths):
    row_count = table.shape[0]
    pages = jnp.take(pool, table, axis=0)
    pages = jnp.swapaxes(pages, 1, 2).reshape(row_count, 2, -1, pool.shape[3], pool.shape[4]).astype(jnp.float32)
    scaling = pool.shape[-1] ** -0.5
    scores = jnp.einsum('bshgd,bthd->bshgt', query_f, pages[:, 0], precision=PRECISE) * scaling
    token_ids = jnp.arange(pages.shape[2], dtype=jnp.int32)
    allowed = (token_ids[None, :] < lengths[:, None])[:, None, None, None, :]
    scores = jnp.where(allowed, scores, NEGATIVE)
    row_top = jnp.max(scores, -1)
    weights_f = jnp.where(allowed, jnp.exp(scores - row_top[..., None]), 0.0)
    blended = jnp.einsum('bshgt,bthd->bshgd', weights_f, pages[:, 1], precision=PRECISE)
    return row_top, jnp.sum(weights_f, -1), blended


def fresh_partial(query_f, fresh):
    fresh_f = fresh.astype(jnp.float32)
    scaling = fresh.shape[-1] ** -0.5
    scores = jnp.einsum('bshgd,bthd->bshgt', query_f, fresh_f[:, :, 0], precision=PRECISE) * scaling
    step_ids = jnp.arange(fresh.shape[1], dtype=jnp.int32)
    allowed = (step_ids[None, :] <= step_ids[:, None])[None, :, None, None, :]
    scores = jnp.where(allowed, scores, NEGATIVE)
    row_top = jnp.max(scores, -1)
    weights_f = jnp.where(allowed, jnp.exp(scores - row_top[..., None]), 0.0)
    blended = jnp.einsum('bshgt,bthd->bshgd', weights_f, fresh_f[:, :, 1], precision=PRECISE)
    return row_top, jnp.sum(weights_f, -1), blended


def page_partial(query_f, page_keys, page_values, row_tag, counts):
    row_count = query_f.shape[0]
    page_size = page_keys.shape[1]
    scaling = page_keys.shape[-1] ** -0.5
    safe_tag = jnp.maximum(row_tag, 0)
    picked = jnp.take(query_f, safe_tag, axis=0)
    scores = jnp.einsum('rshgd,rthd->rshgt', picked, page_keys.astype(jnp.float32), precision=PRECISE) * scaling
    token_ids = jnp.arange(page_size, dtype=jnp.int32)
    allowed = (token_ids[None, :] < counts[:, None]) & (row_tag >= 0)[:, None]
    allowed = allowed[:, None, None, None, :]
    scores = jnp.where(allowed, scores, NEGATIVE)
    page_top = jnp.max(scores, -1)
    member = row_tag[None, :] == jnp.arange(row_count, dtype=jnp.int32)[:, None]
    row_top = jnp.max(jnp.where(member[:, :, None, None, None], page_top[None], NEGATIVE), axis=1)
    weights_f = jnp.where(allowed, jnp.exp(scores - jnp.take(row_top, safe_tag, axis=0)[..., None]), 0.0)
    member_f = member.astype(jnp.float32)
    totals = jnp.einsum('br,rshg->bshg', member_f, jnp.sum(weights_f, -1), precision=PRECISE)
    blended = jnp.einsum('rshgt,rthd->rshgd', weights_f, page_values.astype(jnp.float32), precision=PRECISE)
    blended = jnp.einsum('br,rshgd->bshgd', member_f, blended, precision=PRECISE)
    return row_top, totals, blended


def decode_single(inst_id, queries, fresh, pool, table_flat, lengths, all_kv, all_len, all_dest, all_row):
    row_count, step_count, head_count, row_width = queries.shape
    head_dim = pool.shape[-1]
    page_size = pool.shape[2]
    query_f = queries.reshape(row_count, step_count, head_count, row_width // head_dim, head_dim).astype(jnp.float32)
    table = table_flat.reshape(row_count, -1)
    state = combine(cache_partial(query_f, pool, table, lengths), fresh_partial(query_f, fresh))
    sources = all_kv.shape[0]
    per_span = all_kv.shape[2] // page_size
    page_keys = all_kv[:, 0].reshape(sources * per_span, page_size, head_count, head_dim)
    page_values = all_kv[:, 1].reshape(sources * per_span, page_size, head_count, head_dim)
    starts = jnp.arange(per_span, dtype=jnp.int32) * page_size
    counts = jnp.clip(all_len[:, None] - starts[None, :], 0, page_size).reshape(-1)
    row_tag = jnp.where(all_dest[:, :, 0] == inst_id, all_row, -1).reshape(-1)
    state = combine(state, page_partial(query_f, page_keys, page_values, row_tag, counts))
    row_top, totals, blended = state
    result = blended / totals[..., None]
    return result.reshape(row_count, step_count, head_count, row_width).astype(jnp.bfloat16)


def reference(prefill_q, prefill_kv, span_len, page_seg, page_dest, page_row, dec_q, dec_new, cache_kv, block_table, cache_len):
    prefill_out = lax.map(lambda item: prefill_single(item[0], item[1], item[2], item[3]),
                          (prefill_q, prefill_kv, span_len, page_seg))
    inst_ids = jnp.arange(prefill_q.shape[0], dtype=jnp.int32)

    def decode_item(item):
        return decode_single(item[0], item[1], item[2], item[3], item[4], item[5],
                             prefill_kv, span_len, page_dest, page_row)

    dec_out = lax.map(decode_item, (inst_ids, dec_q, dec_new, cache_kv, block_table, cache_len))
    return prefill_out, dec_out
```

```python
import functools
import math

import jax
import jax.numpy as jnp
from jax import lax
from jax.experimental import pallas as pl
from jax.experimental.pallas import tpu as pltpu
from jax.sharding import PartitionSpec as P

NEGATIVE = -1e30
LOG2E = math.log2(math.e)
LANES = 128
DIRECT = 8
VMEM_LIMIT = 48 * 1024 * 1024

SMEM_SPEC = pl.BlockSpec(memory_space=pltpu.SMEM)
VMEM_SPEC = pl.BlockSpec(memory_space=pltpu.VMEM)


def query_rows(field):
    lead = math.prod(field.shape[:-2])
    heads, width = field.shape[-2:]
    split = field.reshape(lead, heads, width // LANES, LANES)
    return split.transpose(0, 2, 1, 3).reshape(-1, LANES)


def from_rows(rows, shape):
    heads, width = shape[-2:]
    lead = math.prod(shape[:-2])
    split = rows.reshape(lead, width // LANES, heads, LANES)
    return split.transpose(0, 2, 1, 3).reshape(shape)


def head_of(shape, axis, heads):
    return lax.broadcasted_iota(jnp.int32, shape, axis) % heads


def dot_nt(first, second):
    return lax.dot_general(
        first, second, (((1,), (1,)), ((), ())), preferred_element_type=jnp.float32
    )


def dot_nn(first, second):
    return jnp.dot(first, second, preferred_element_type=jnp.float32)


def two_terms(weights):
    upper = weights.astype(jnp.bfloat16)
    lower = (weights - upper.astype(jnp.float32)).astype(jnp.bfloat16)
    return jnp.concatenate([upper, lower], axis=0)


def spread_heads(rows, heads):
    if heads == 1:
        return rows
    owner = head_of(rows.shape, 0, heads)
    zero = jnp.zeros_like(rows)
    return jnp.concatenate([jnp.where(owner == h, rows, zero) for h in range(heads)], axis=1)


def pick_head(wide, heads):
    if heads == 1:
        return wide
    owner = head_of((wide.shape[0], LANES), 0, heads)
    picked = wide[:, :LANES]
    for h in range(1, heads):
        picked = jnp.where(owner == h, wide[:, h * LANES : (h + 1) * LANES], picked)
    return picked


def cache_kernel(
    sizes, seg_ref, dest_ref, row_ref, len_ref, table_ref, clen_ref,
    q_ref, fresh_ref, pool_ref, kv_ref,
    info_ref, part_ref, lse_ref, keys_ref, vals_ref,
    scr_ref, fscr_ref,
):
    heads, page, pages, rows, steps, pages_max, requests = sizes
    span = pages * page
    length = len_ref[0]

    for r in range(info_ref.shape[1]):
        for f in range(4):
            info_ref[f, r] = 0

    def note(p, _):
        r = seg_ref[0, p]
        fresh_request = jnp.logical_or(p == 0, r != seg_ref[0, jnp.maximum(p - 1, 0)])

        @pl.when(fresh_request)
        def _():
            info_ref[0, r] = p * page
            info_ref[2, r] = dest_ref[0, p]
            info_ref[3, r] = row_ref[0, p]

        info_ref[1, r] = jnp.minimum((p + 1) * page, length)
        return 0

    lax.fori_loop(0, pages, note, 0)

    for part, out_ref in enumerate((keys_ref, vals_ref)):
        if heads == 1:
            out_ref[...] = kv_ref[part * span : (part + 1) * span, :]
        else:
            scr_ref[...] = kv_ref[part * span * heads : (part + 1) * span * heads, :].astype(
                jnp.float32
            )
            for h in range(heads):
                out_ref[:, h * LANES : (h + 1) * LANES] = scr_ref[
                    pl.ds(h, span, stride=heads), :
                ].astype(jnp.bfloat16)

    scale2 = LANES**-0.5 * LOG2E
    per_row = q_ref.shape[0] // rows
    groups = per_row // (steps * heads)
    fresh_rows = fresh_ref.shape[0]
    fscr_ref[...] = jnp.zeros_like(fscr_ref)
    fscr_ref[:fresh_rows, :] = fresh_ref[...]
    fresh = fscr_ref[...]
    width = fresh.shape[0]
    page_rows = page * heads

    col = lax.broadcasted_iota(jnp.int32, (per_row, width), 1)
    sub = lax.broadcasted_iota(jnp.int32, (per_row, width), 0)
    fresh_ok = (
        ((col // heads) % 2 == 0)
        & ((col // (2 * heads)) % steps <= sub // (groups * heads))
        & (col % heads == sub % heads)
    )
    col_row = col // (2 * heads * steps)
    ccol = lax.broadcasted_iota(jnp.int32, (per_row, pages_max * page_rows), 1)
    csub = lax.broadcasted_iota(jnp.int32, (per_row, pages_max * page_rows), 0)
    same_head = ccol % heads == csub % heads
    ctok = ccol // heads

    for b in range(rows):
        q_b = q_ref[b * per_row : (b + 1) * per_row, :]
        tables = [table_ref[0, b * pages_max + j] for j in range(pages_max)]

        def gather(part):
            pieces = [
                pool_ref[
                    pl.ds(pl.multiple_of((t * 2 + part) * page_rows, page_rows), page_rows), :
                ]
                for t in tables
            ]
            return jnp.concatenate(pieces, axis=0)

        s_c = dot_nt(q_b, gather(0))
        s_f = dot_nt(q_b, fresh)
        keep_c = same_head & (ctok < clen_ref[0, b])
        keep_f = fresh_ok & (col_row == b)
        s_c = jnp.where(keep_c, s_c, NEGATIVE)
        s_f = jnp.where(keep_f, s_f, NEGATIVE)
        top = jnp.maximum(
            jnp.max(s_c, axis=1, keepdims=True), jnp.max(s_f, axis=1, keepdims=True)
        )
        w_c = jnp.where(keep_c, jnp.exp2((s_c - top) * scale2), 0.0)
        w_f = jnp.where(keep_f, jnp.exp2((s_f - top) * scale2), 0.0)
        total = jnp.sum(w_c, axis=1, keepdims=True) + jnp.sum(w_f, axis=1, keepdims=True)
        acc = dot_nn(two_terms(w_c), gather(1))
        acc = acc + dot_nn(two_terms(pltpu.roll(w_f, heads, 1)), fresh)
        blended = acc[:per_row] + acc[per_row:]
        part_ref[b * per_row : (b + 1) * per_row, :] = blended / total
        lse = top * scale2 + jnp.log2(total)
        lse_ref[b * per_row : (b + 1) * per_row, :] = jnp.broadcast_to(lse, (per_row, LANES))


def pages_kernel(sizes, per_slot, info_ref, *refs):
    heads, page, pages, rows, steps, pages_max, requests, instances = sizes
    slot_count = instances // per_slot
    slots = refs[:slot_count]
    keys_ref, vals_ref, own_ref, send_ref, q_scr = refs[slot_count:]
    me = lax.axis_index("inst")
    per_row = slots[0].shape[0] // (per_slot * rows)
    span = pages * page
    scale2 = LANES**-0.5 * LOG2E
    for r in range(requests):
        slot = lax.rem(me - info_ref[2, r] + instances, instances)
        row = info_ref[3, r]
        if slot_count == 1:
            start = pl.multiple_of((slot * rows + row) * per_row, per_row)
            q_scr[r * per_row : (r + 1) * per_row, :] = slots[0][pl.ds(start, per_row), :]
        else:
            start = pl.multiple_of(row * per_row, per_row)
            for k in range(slot_count):

                @pl.when(slot == k)
                def _():
                    q_scr[r * per_row : (r + 1) * per_row, :] = slots[k][pl.ds(start, per_row), :]

    scores = dot_nt(spread_heads(q_scr[...], heads), keys_ref[...])
    token = lax.broadcasted_iota(jnp.int32, (per_row, span), 1)
    weights, tops, totals = [], [], []
    for r in range(requests):
        keep = (token >= info_ref[0, r]) & (token < info_ref[1, r])
        s_r = jnp.where(keep, scores[r * per_row : (r + 1) * per_row], NEGATIVE)
        top = jnp.max(s_r, axis=1, keepdims=True)
        w_r = jnp.where(keep, jnp.exp2((s_r - top) * scale2), 0.0)
        weights.append(w_r)
        tops.append(top)
        totals.append(jnp.sum(w_r, axis=1, keepdims=True))
    count = requests * per_row
    acc = dot_nn(two_terms(jnp.concatenate(weights, axis=0)), vals_ref[...])
    acc = pick_head(acc[:count] + acc[count:], heads)
    total = jnp.concatenate(totals, axis=0)
    live = total > 0.0
    blended = jnp.where(live, acc / jnp.where(live, total, 1.0), 0.0)
    lse = jnp.where(
        live,
        jnp.concatenate(tops, axis=0) * scale2 + jnp.log2(jnp.where(live, total, 1.0)),
        NEGATIVE,
    )
    own_ref[...] = blended
    send_ref[:count, :] = blended.astype(jnp.bfloat16)
    blocks = -(-count // LANES)
    lines = []
    for j in range(blocks):
        piece = lse[j * LANES : min((j + 1) * LANES, count)]
        shape = (piece.shape[0], LANES)
        same = lax.broadcasted_iota(jnp.int32, shape, 0) == lax.broadcasted_iota(
            jnp.int32, shape, 1
        )
        lines.append(jnp.sum(jnp.where(same, piece, 0.0), axis=0, keepdims=True))
    line = jnp.concatenate(lines, axis=0)
    first = line.astype(jnp.bfloat16)
    rest = line - first.astype(jnp.float32)
    second = rest.astype(jnp.bfloat16)
    third = (rest - second.astype(jnp.float32)).astype(jnp.bfloat16)
    spare = send_ref.shape[0] - count
    terms = [t.astype(jnp.float32) for t in (first, second, third)]
    terms.append(jnp.zeros((spare - 3 * blocks, LANES), jnp.float32))
    send_ref[count:, :] = jnp.concatenate(terms, axis=0).astype(jnp.bfloat16)


def prefill_kernel(sizes, seg_ref, info_ref, len_ref, q_ref, keys_ref, vals_ref, after_ref, out_ref, lag_ref):
    heads, page, pages, block = sizes
    tile = pl.program_id(0)
    page_rows = out_ref.shape[0] * page // block
    per_token = page_rows // page
    per_block = block // page
    scale2 = LANES**-0.5 * LOG2E
    length = len_ref[0]

    @pl.when(tile == 0)
    def _():
        lane = lax.broadcasted_iota(jnp.int32, lag_ref.shape, 1)
        lag_ref[...] = lane - lax.broadcasted_iota(jnp.int32, lag_ref.shape, 0) // per_token

    first_key = info_ref[0, seg_ref[0, tile * per_block]]
    first_block = first_key // block
    behind = tile - first_block

    def attend(count):
        base = (tile - (count - 1)) * block
        keys = keys_ref[pl.ds(pl.multiple_of(base, block), count * block), :]
        vals = vals_ref[pl.ds(pl.multiple_of(base, block), count * block), :]
        lane = lax.broadcasted_iota(jnp.int32, (1, block), 1)
        for p in range(per_block):
            rows = slice(p * page_rows, (p + 1) * page_rows)
            scores = dot_nt(spread_heads(q_ref[rows, :], heads), keys)
            start = info_ref[0, seg_ref[0, tile * per_block + p]] - base
            pieces = []
            for j in range(count):
                s_j = scores[:, j * block : (j + 1) * block]
                keep = lane >= start - j * block
                if j == count - 1:
                    keep = keep & (lag_ref[...] <= p * page)
                pieces.append(jnp.where(keep, s_j, NEGATIVE))
            top = pieces[0]
            for piece in pieces[1:]:
                top = jnp.maximum(top, piece)
            top = jnp.max(top, axis=1, keepdims=True)
            weights = [jnp.exp2((piece - top) * scale2) for piece in pieces]
            total = weights[0]
            for w_j in weights[1:]:
                total = total + w_j
            total = jnp.sum(total, axis=1, keepdims=True)
            joined = jnp.concatenate([w_j.astype(jnp.bfloat16) for w_j in weights], axis=1)
            acc = pick_head(dot_nn(joined, vals), heads)
            place = lax.broadcasted_iota(jnp.int32, (page_rows, 1), 0) // per_token
            live = place < length - (tile * block + p * page)
            out_ref[rows, :] = (acc * jnp.where(live, 1.0 / total, 0.0)).astype(jnp.bfloat16)

    longest = 3
    for count in range(1, longest + 1):
        pl.when(behind == count - 1)(functools.partial(attend, count))


def join_kernel(sizes, per_slot, *refs):
    heads, rows, requests, instances = sizes
    slot_count = instances // per_slot
    infos = refs[:slot_count]
    own_ref = refs[slot_count]
    sent = refs[slot_count + 1 : 2 * slot_count + 1]
    part_ref, lse_ref, out_ref, top_scr, total_scr, acc_scr = refs[2 * slot_count + 1 :]
    me = lax.axis_index("inst")
    per_row = part_ref.shape[0] // rows
    count = requests * per_row
    blocks = -(-count // LANES)
    top_scr[...] = lse_ref[...]
    total_scr[...] = jnp.ones_like(total_scr)
    acc_scr[...] = part_ref[...]
    lane = lax.broadcasted_iota(jnp.int32, (per_row, LANES), 1)
    sub = lax.broadcasted_iota(jnp.int32, (per_row, LANES), 0)

    def absorb(slot_ref, info_ref, line, index, values_ref):
        for r in range(requests):

            @pl.when(jnp.logical_and(info_ref[index * 4 + 2, r] == me, info_ref[index * 4 + 1, r] > info_ref[index * 4, r]))
            def _():
                place = pl.ds(pl.multiple_of(info_ref[index * 4 + 3, r] * per_row, per_row), per_row)
                j, offset = divmod(r * per_row, LANES)
                spread = jnp.where(lane == sub + offset, line[j : j + 1, :], 0.0)
                level = jnp.sum(spread, axis=1, keepdims=True)
                top = top_scr[place, :]
                joined = jnp.maximum(top, level)
                old = jnp.exp2(top - joined)
                new = jnp.exp2(level - joined)
                values = values_ref(r)
                top_scr[place, :] = joined
                total_scr[place, :] = total_scr[place, :] * old + new
                acc_scr[place, :] = acc_scr[place, :] * old + values * new

    for k in range(slot_count):
        tall = sent[k].shape[0] // per_slot
        for i in range(per_slot):
            base = i * tall
            stats = sent[k][base + count : base + tall, :].astype(jnp.float32)
            line = stats[:blocks] + stats[blocks : 2 * blocks] + stats[2 * blocks : 3 * blocks]

            def values_ref(r, k=k, i=i, base=base):
                if k == 0 and i == 0:
                    return own_ref[r * per_row : (r + 1) * per_row, :]
                spot = base + r * per_row
                return sent[k][spot : spot + per_row, :].astype(jnp.float32)

            absorb(sent[k], infos[k], line, i, values_ref)
    out_ref[...] = (acc_scr[...] / total_scr[...]).astype(jnp.bfloat16)


def exchange(block, instances):
    if instances <= DIRECT:
        slots = [block]
        for k in range(1, instances):
            slots.append(
                lax.ppermute(block, "inst", [(i, (i + k) % instances) for i in range(instances)])
            )
        return slots
    whole = lax.all_gather(block, "inst", axis=0)
    order = lax.rem(lax.axis_index("inst") - jnp.arange(instances) + instances, instances)
    return [jnp.take(whole, order, axis=0).reshape((-1,) + block.shape[1:])]


def params(**extra):
    return pltpu.CompilerParams(vmem_limit_bytes=VMEM_LIMIT, **extra)


def shards(
    instances,
    prefill_q,
    prefill_kv,
    span_len,
    page_seg,
    page_dest,
    page_row,
    dec_q,
    dec_new,
    cache_kv,
    block_table,
    cache_len,
):
    _, span, heads, width = prefill_q.shape
    pages = page_seg.shape[1]
    _, rows, steps = dec_q.shape[:3]
    pool, page = cache_kv.shape[1], cache_kv.shape[3]
    pages_max = block_table.shape[1] // rows
    capacity = -(-2 * pages // instances)
    requests = pages - capacity + 1
    groups = width // LANES
    per_row = steps * groups * heads
    block = LANES
    sizes = (heads, page, pages, rows, steps, pages_max, requests)
    dest = page_dest.reshape(1, pages)
    slot_width = 32
    f32, bf16, i32 = jnp.float32, jnp.bfloat16, jnp.int32
    shape = jax.ShapeDtypeStruct

    queries = query_rows(dec_q[0])
    q_slots = exchange(queries, instances)
    per_slot = instances // len(q_slots)

    info, part, lse, keys, vals = pl.pallas_call(
        functools.partial(cache_kernel, sizes),
        out_shape=(
            shape((4, slot_width), i32),
            shape((rows * per_row, LANES), f32),
            shape((rows * per_row, LANES), f32),
            shape((span, heads * LANES), bf16),
            shape((span, heads * LANES), bf16),
        ),
        in_specs=[SMEM_SPEC] * 6 + [VMEM_SPEC] * 4,
        out_specs=(SMEM_SPEC,) + (VMEM_SPEC,) * 4,
        scratch_shapes=[
            pltpu.VMEM((span * heads, LANES), f32),
            pltpu.VMEM((-(-dec_new[0].size // LANES // LANES) * LANES, LANES), bf16),
        ],
        compiler_params=params(),
        name="cache",
    )(
        page_seg, dest, page_row, span_len, block_table, cache_len,
        queries, dec_new.reshape(-1, LANES), cache_kv.reshape(-1, LANES),
        prefill_kv.reshape(-1, LANES),
    )
    info_slots = exchange(info, instances)

    count = requests * per_row
    tall = count + -(-3 * -(-count // LANES) // 16) * 16
    own, sent = pl.pallas_call(
        functools.partial(pages_kernel, sizes + (instances,), per_slot),
        out_shape=(shape((count, LANES), f32), shape((tall, LANES), bf16)),
        in_specs=[SMEM_SPEC] + [VMEM_SPEC] * (len(q_slots) + 2),
        out_specs=(VMEM_SPEC, VMEM_SPEC),
        scratch_shapes=[pltpu.VMEM((count, LANES), bf16)],
        compiler_params=params(),
        name="pages",
    )(info, *q_slots, keys, vals)
    sent_slots = exchange(sent, instances)

    q_rows = query_rows(prefill_q[0])
    tile_rows = block * groups * heads
    tiles = span // block
    whole = lambda i: (0, 0)
    prefill_out = pl.pallas_call(
        functools.partial(prefill_kernel, (heads, page, pages, block)),
        out_shape=shape(q_rows.shape, bf16),
        grid=(tiles,),
        in_specs=[SMEM_SPEC] * 3
        + [
            pl.BlockSpec((tile_rows, LANES), lambda i: (i, 0)),
            pl.BlockSpec(keys.shape, whole),
            pl.BlockSpec(vals.shape, whole),
            pl.BlockSpec(memory_space=pl.ANY),
        ],
        out_specs=pl.BlockSpec((tile_rows, LANES), lambda i: (i, 0)),
        scratch_shapes=[pltpu.VMEM((page * groups * heads, block), i32)],
        compiler_params=params(),
        name="prefill",
    )(page_seg, info, span_len, q_rows, keys, vals, own)

    dec_out = pl.pallas_call(
        functools.partial(join_kernel, (heads, rows, requests, instances), per_slot),
        out_shape=shape((rows * per_row, LANES), bf16),
        in_specs=[SMEM_SPEC] * len(info_slots) + [VMEM_SPEC] * (3 + len(sent_slots)),
        out_specs=VMEM_SPEC,
        scratch_shapes=[pltpu.VMEM((rows * per_row, LANES), f32)] * 3,
        compiler_params=params(),
        name="join",
    )(*info_slots, own, *sent_slots, part, lse)

    return (
        from_rows(prefill_out, prefill_q.shape),
        from_rows(dec_out, dec_q.shape),
    )


def solution(mesh):
    return jax.shard_map(
        functools.partial(shards, mesh.shape["inst"]),
        mesh=mesh,
        in_specs=(
            P(("pool", "inst"), None, "tp", None),
            P(("pool", "inst"), None, None, "tp", None),
            P(("pool", "inst")),
            P(("pool", "inst"), None),
            P(("pool", "inst"), None, None),
            P(("pool", "inst"), None),
            P(("pool", "inst"), None, None, "tp", None),
            P(("pool", "inst"), None, None, None, "tp", None),
            P(("pool", "inst"), None, None, None, "tp", None),
            P(("pool", "inst"), None),
            P(("pool", "inst"), None),
        ),
        out_specs=(
            P(("pool", "inst"), None, "tp", None),
            P(("pool", "inst"), None, None, "tp", None),
        ),
        check_vma=False,
    )
```

```python
import functools
import math

import jax
import jax.numpy as jnp
from jax import lax
from jax.experimental import pallas as pl
from jax.experimental.pallas import tpu as pltpu
from jax.sharding import PartitionSpec as P

NEGATIVE = -1e30
LOG2E = math.log2(math.e)
LANES = 128
DIRECT = 8
VMEM_LIMIT = 48 * 1024 * 1024

SMEM_SPEC = pl.BlockSpec(memory_space=pltpu.SMEM)
HBM_SPEC = pl.BlockSpec(memory_space=pltpu.HBM)
VMEM_SPEC = pl.BlockSpec(memory_space=pltpu.VMEM)


def query_rows(field):
    lead = math.prod(field.shape[:-2])
    heads, width = field.shape[-2:]
    split = field.reshape(lead, heads, width // LANES, LANES)
    return split.transpose(0, 2, 1, 3).reshape(-1, LANES)


def from_rows(rows, shape):
    heads, width = shape[-2:]
    lead = math.prod(shape[:-2])
    split = rows.reshape(lead, width // LANES, heads, LANES)
    return split.transpose(0, 2, 1, 3).reshape(shape)


def head_of(shape, axis, heads):
    return lax.broadcasted_iota(jnp.int32, shape, axis) % heads


def dot_nt(first, second):
    return lax.dot_general(
        first, second, (((1,), (1,)), ((), ())), preferred_element_type=jnp.float32
    )


def dot_nn(first, second):
    return jnp.dot(first, second, preferred_element_type=jnp.float32)


def two_terms(weights):
    upper = weights.astype(jnp.bfloat16)
    lower = (weights - upper.astype(jnp.float32)).astype(jnp.bfloat16)
    return jnp.concatenate([upper, lower], axis=0)


def spread_heads(rows, heads):
    if heads == 1:
        return rows
    owner = head_of((16, LANES), 0, heads)
    tall = rows.reshape(-1, 16, LANES)
    parts = []
    for h in range(heads):
        mark = jnp.where(owner == h, 1.0, 0.0).astype(rows.dtype)
        parts.append((tall * mark[None]).reshape(rows.shape))
    return jnp.concatenate(parts, axis=1)


def pick_head(wide, heads):
    if heads == 1:
        return wide
    owner = head_of((wide.shape[0], LANES), 0, heads)
    picked = wide[:, :LANES]
    for h in range(1, heads):
        picked = jnp.where(owner == h, wide[:, h * LANES : (h + 1) * LANES], picked)
    return picked


def cache_kernel(
    sizes, seg_hbm, dest_hbm, row_hbm, len_hbm, table_hbm, clen_hbm,
    q_hbm, fresh_hbm, pool_hbm, kv_hbm,
    info_ref, part_ref, lse_ref, keys_ref, vals_ref, own_q_ref,
    seg_ref, dest_ref, row_ref, len_ref, table_ref, clen_ref,
    fresh_ref, pool_ref, kv_ref, scr_ref, sems,
):
    heads, page, pages, rows, steps, pages_max, requests = sizes
    copies = [
        pltpu.make_async_copy(source, target, sems.at[i])
        for i, (source, target) in enumerate((
            (seg_hbm, seg_ref), (dest_hbm, dest_ref), (row_hbm, row_ref), (len_hbm, len_ref),
            (kv_hbm, kv_ref), (table_hbm, table_ref), (clen_hbm, clen_ref),
            (q_hbm, own_q_ref), (fresh_hbm, fresh_ref.at[: fresh_hbm.shape[0]]),
            (pool_hbm, pool_ref),
        ))
    ]
    if fresh_ref.shape[0] > fresh_hbm.shape[0]:
        fresh_ref[fresh_hbm.shape[0] :, :] = jnp.zeros(
            (fresh_ref.shape[0] - fresh_hbm.shape[0], LANES), fresh_ref.dtype
        )
    for copy in copies:
        copy.start()
    span = pages * page

    for r in range(info_ref.shape[1]):
        info_ref[0, r] = 0
        info_ref[1, r] = 0
        info_ref[2, r] = -1
        info_ref[3, r] = 0
    for copy in copies[:4]:
        copy.wait()
    length = len_ref[0]
    info_ref[5, 0] = length

    def note(p, _):
        r = seg_ref[0, p]
        fresh_request = jnp.logical_or(p == 0, r != seg_ref[0, jnp.maximum(p - 1, 0)])

        @pl.when(fresh_request)
        def _():
            info_ref[0, r] = p * page
            info_ref[2, r] = jnp.where(p * page < length, dest_ref[0, p], -1)
            info_ref[3, r] = row_ref[0, p]

        info_ref[1, r] = jnp.minimum((p + 1) * page, length)
        info_ref[4, p] = info_ref[0, r]
        return 0

    lax.fori_loop(0, pages, note, 0)

    copies[4].wait()
    for part, out_ref in enumerate((keys_ref, vals_ref)):
        if heads == 1:
            out_ref[...] = kv_ref[part * span : (part + 1) * span, :]
        else:
            scr_ref[...] = kv_ref[part * span * heads : (part + 1) * span * heads, :].astype(
                jnp.float32
            )
            for h in range(heads):
                out_ref[:, h * LANES : (h + 1) * LANES] = scr_ref[
                    pl.ds(h, span, stride=heads), :
                ].astype(jnp.bfloat16)

    for copy in copies[5:]:
        copy.wait()
    scale2 = LANES**-0.5 * LOG2E
    per_row = own_q_ref.shape[0] // rows
    groups = per_row // (steps * heads)
    fresh = fresh_ref[...]
    width = fresh.shape[0]
    page_rows = page * heads

    col = lax.broadcasted_iota(jnp.int32, (per_row, width), 1)
    sub = lax.broadcasted_iota(jnp.int32, (per_row, width), 0)
    fresh_ok = (
        ((col // heads) % 2 == 0)
        & ((col // (2 * heads)) % steps <= sub // (groups * heads))
        & (col % heads == sub % heads)
    )
    fresh_row = jnp.where(fresh_ok, col // (2 * heads * steps), -1)
    ccol = lax.broadcasted_iota(jnp.int32, (per_row, pages_max * page_rows), 1)
    csub = lax.broadcasted_iota(jnp.int32, (per_row, pages_max * page_rows), 0)
    far = rows * pages_max * page
    token = jnp.where(ccol % heads == csub % heads, ccol // heads, far)

    def gather(b, part):
        pieces = []
        for j in range(pages_max):
            spot = (table_ref[0, b * pages_max + j] * 2 + part) * page_rows
            pieces.append(pool_ref[pl.ds(pl.multiple_of(spot, page_rows), page_rows), :])
        return jnp.concatenate(pieces, axis=0)

    def row_slice(b):
        return slice(b * per_row, (b + 1) * per_row)

    fresh_scores = [dot_nt(own_q_ref[row_slice(b), :], fresh) for b in range(rows)]
    scores = [dot_nt(own_q_ref[row_slice(b), :], gather(b, 0)) for b in range(rows)]
    cache_terms, fresh_terms, totals = [], [], []
    for b in range(rows):
        s_c = jnp.where(token < clen_ref[0, b], scores[b], NEGATIVE)
        s_f = jnp.where(fresh_row == b, fresh_scores[b], NEGATIVE)
        pieces = [s_c[:, i : i + width] for i in range(0, s_c.shape[1], width)] + [s_f]
        top = functools.reduce(jnp.maximum, pieces)
        top = jnp.max(top, axis=1, keepdims=True)
        weights = [jnp.exp2((piece - top) * scale2) for piece in pieces]
        total = jnp.sum(functools.reduce(jnp.add, weights), axis=1, keepdims=True)
        cache_terms.append(two_terms(jnp.concatenate(weights[:-1], axis=1)))
        fresh_terms.append(pltpu.roll(weights[-1], heads, 1))
        totals.append(total)
        lse = top * scale2 + jnp.log2(total)
        lse_ref[row_slice(b), :] = jnp.broadcast_to(lse, (per_row, LANES))
    count = rows * per_row
    fresh_acc = dot_nn(two_terms(jnp.concatenate(fresh_terms, axis=0)), fresh)
    fresh_acc = fresh_acc[:count] + fresh_acc[count:]
    for b in range(rows):
        acc = dot_nn(cache_terms[b], gather(b, 1))
        acc = acc[:per_row] + acc[per_row:] + fresh_acc[row_slice(b)]
        part_ref[row_slice(b), :] = acc * (1.0 / totals[b])


def pages_kernel(sizes, per_slot, info_ref, *refs):
    heads, page, pages, rows, steps, pages_max, requests, instances = sizes
    slot_count = instances // per_slot
    slots = refs[:slot_count]
    keys_ref, vals_ref, own_ref, send_ref, q_scr = refs[slot_count:]
    me = lax.axis_index("inst")
    per_row = slots[0].shape[0] // (per_slot * rows)
    span = pages * page
    scale2 = LANES**-0.5 * LOG2E
    for r in range(requests):
        slot = lax.rem(me - info_ref[2, r] + instances, instances)
        row = info_ref[3, r]
        if slot_count == 1:
            start = pl.multiple_of((slot * rows + row) * per_row, per_row)
            q_scr[r * per_row : (r + 1) * per_row, :] = slots[0][pl.ds(start, per_row), :]
        else:
            start = pl.multiple_of(row * per_row, per_row)
            for k in range(slot_count):

                @pl.when(slot == k)
                def _():
                    q_scr[r * per_row : (r + 1) * per_row, :] = slots[k][pl.ds(start, per_row), :]

    scores = dot_nt(spread_heads(q_scr[...], heads), keys_ref[...])
    token = lax.broadcasted_iota(jnp.int32, (per_row, span), 1)
    weights, tops, totals = [], [], []
    for r in range(requests):
        keep = (token >= info_ref[0, r]) & (token < info_ref[1, r])
        s_r = jnp.where(keep, scores[r * per_row : (r + 1) * per_row], NEGATIVE)
        top = jnp.max(s_r, axis=1, keepdims=True)
        w_r = jnp.where(keep, jnp.exp2((s_r - top) * scale2), 0.0)
        weights.append(w_r)
        tops.append(top)
        totals.append(jnp.sum(w_r, axis=1, keepdims=True))
    count = requests * per_row
    acc = dot_nn(two_terms(jnp.concatenate(weights, axis=0)), vals_ref[...])
    acc = pick_head(acc[:count] + acc[count:], heads)
    total = jnp.concatenate(totals, axis=0)
    live = total > 0.0
    blended = jnp.where(live, acc / jnp.where(live, total, 1.0), 0.0)
    lse = jnp.where(
        live,
        jnp.concatenate(tops, axis=0) * scale2 + jnp.log2(jnp.where(live, total, 1.0)),
        NEGATIVE,
    )
    own_ref[...] = blended
    send_ref[:count, :] = blended.astype(jnp.bfloat16)
    blocks = -(-count // LANES)
    lines = []
    for j in range(blocks):
        piece = lse[j * LANES : min((j + 1) * LANES, count)]
        shape = (piece.shape[0], LANES)
        same = lax.broadcasted_iota(jnp.int32, shape, 0) == lax.broadcasted_iota(
            jnp.int32, shape, 1
        )
        lines.append(jnp.sum(jnp.where(same, piece, 0.0), axis=0, keepdims=True))
    line = jnp.concatenate(lines, axis=0)
    first = line.astype(jnp.bfloat16)
    rest = line - first.astype(jnp.float32)
    second = rest.astype(jnp.bfloat16)
    third = (rest - second.astype(jnp.float32)).astype(jnp.bfloat16)
    terms = [t.astype(jnp.float32) for t in (first, second, third)]
    lane = lax.broadcasted_iota(jnp.int32, (1, LANES), 1)
    for f in (2, 3):
        tags = jnp.full((1, LANES), -1, jnp.int32)
        for r in range(requests):
            tags = jnp.where(lane == r, info_ref[f, r], tags)
        terms.append(tags.astype(jnp.float32))
    spare = send_ref.shape[0] - count
    terms.append(jnp.zeros((spare - 3 * blocks - 2, LANES), jnp.float32))
    send_ref[count:, :] = jnp.concatenate(terms, axis=0).astype(jnp.bfloat16)


def prefill_kernel(sizes, info_ref, q_ref, keys_ref, vals_ref, after_ref, out_ref, lag_ref):
    heads, page, pages, block = sizes
    tile = pl.program_id(0)
    page_rows = out_ref.shape[0] * page // block
    per_token = page_rows // page
    per_block = block // page
    scale2 = LANES**-0.5 * LOG2E
    length = info_ref[5, 0]

    @pl.when(tile == 0)
    def _():
        lane = lax.broadcasted_iota(jnp.int32, lag_ref.shape, 1)
        lag_ref[...] = lane - lax.broadcasted_iota(jnp.int32, lag_ref.shape, 0) // per_token

    first_key = info_ref[4, tile * per_block]
    first_block = first_key // block
    behind = tile - first_block

    def attend(count):
        base = (tile - (count - 1)) * block
        keys = keys_ref[pl.ds(pl.multiple_of(base, block), count * block), :]
        vals = vals_ref[pl.ds(pl.multiple_of(base, block), count * block), :]
        lane = lax.broadcasted_iota(jnp.int32, (1, block), 1)
        for p in range(per_block):
            rows = slice(p * page_rows, (p + 1) * page_rows)
            scores = dot_nt(spread_heads(q_ref[rows, :], heads), keys)
            start = info_ref[4, tile * per_block + p] - base
            pieces = []
            for j in range(count):
                s_j = scores[:, j * block : (j + 1) * block]
                keep = lane >= start - j * block
                if j == count - 1:
                    keep = keep & (lag_ref[...] <= p * page)
                pieces.append(jnp.where(keep, s_j, NEGATIVE))
            top = pieces[0]
            for piece in pieces[1:]:
                top = jnp.maximum(top, piece)
            top = jnp.max(top, axis=1, keepdims=True)
            weights = [jnp.exp2((piece - top) * scale2) for piece in pieces]
            total = weights[0]
            for w_j in weights[1:]:
                total = total + w_j
            total = jnp.sum(total, axis=1, keepdims=True)
            joined = jnp.concatenate([w_j.astype(jnp.bfloat16) for w_j in weights], axis=1)
            acc = pick_head(dot_nn(joined, vals), heads)
            place = lax.broadcasted_iota(jnp.int32, (page_rows, 1), 0) // per_token
            live = place < length - (tile * block + p * page)
            out_ref[rows, :] = (acc * jnp.where(live, 1.0 / total, 0.0)).astype(jnp.bfloat16)

    longest = 3
    for count in range(1, longest + 1):
        pl.when(behind == count - 1)(functools.partial(attend, count))


def join_kernel(sizes, per_slot, *refs):
    heads, rows, requests, instances = sizes
    slot_count = instances // per_slot
    own_ref = refs[0]
    sent = refs[1 : slot_count + 1]
    part_ref, lse_ref, out_ref, top_scr, total_scr, acc_scr, tag_scr, tags, sem = refs[slot_count + 1 :]
    me = lax.axis_index("inst")
    per_row = part_ref.shape[0] // rows
    count = requests * per_row
    blocks = -(-count // LANES)
    tall = sent[0].shape[0] // per_slot
    lines = []
    for n in range(instances):
        k, i = divmod(n, per_slot)
        stats = sent[k][i * tall + count : (i + 1) * tall, :].astype(jnp.float32)
        lines.append(
            stats[:blocks] + stats[blocks : 2 * blocks] + stats[2 * blocks : 3 * blocks]
        )
        tag_scr[n : n + 1, :] = stats[3 * blocks : 3 * blocks + 1].astype(jnp.int32)
        tag_scr[instances + n : instances + n + 1, :] = stats[
            3 * blocks + 1 : 3 * blocks + 2
        ].astype(jnp.int32)
    copy = pltpu.make_async_copy(tag_scr, tags, sem)
    copy.start()
    top_scr[...] = lse_ref[...]
    total_scr[...] = jnp.ones_like(total_scr)
    acc_scr[...] = part_ref[...]
    lane = lax.broadcasted_iota(jnp.int32, (per_row, LANES), 1)
    sub = lax.broadcasted_iota(jnp.int32, (per_row, LANES), 0)
    copy.wait()
    for n in range(instances):
        k, i = divmod(n, per_slot)
        for r in range(requests):

            @pl.when(tags[n, r] == me)
            def _():
                start = pl.multiple_of(tags[instances + n, r] * per_row, per_row)
                place = pl.ds(start, per_row)
                j, offset = divmod(r * per_row, LANES)
                spread = jnp.where(lane == sub + offset, lines[n][j : j + 1, :], 0.0)
                level = jnp.sum(spread, axis=1, keepdims=True)
                spot = r * per_row
                if n == 0:
                    values = own_ref[spot : spot + per_row, :]
                else:
                    spot = spot + i * tall
                    values = sent[k][spot : spot + per_row, :].astype(jnp.float32)
                top = top_scr[place, :]
                joined = jnp.maximum(top, level)
                old = jnp.exp2(top - joined)
                new = jnp.exp2(level - joined)
                top_scr[place, :] = joined
                total_scr[place, :] = total_scr[place, :] * old + new
                acc_scr[place, :] = acc_scr[place, :] * old + values * new

    out_ref[...] = (acc_scr[...] / total_scr[...]).astype(jnp.bfloat16)


def exchange(block, instances):
    if instances <= DIRECT:
        slots = [block]
        for k in range(1, instances):
            slots.append(
                lax.ppermute(block, "inst", [(i, (i + k) % instances) for i in range(instances)])
            )
        return slots
    whole = lax.all_gather(block, "inst", axis=0)
    order = lax.rem(lax.axis_index("inst") - jnp.arange(instances) + instances, instances)
    return [jnp.take(whole, order, axis=0).reshape((-1,) + block.shape[1:])]


def params(**extra):
    return pltpu.CompilerParams(vmem_limit_bytes=VMEM_LIMIT, **extra)


def shards(
    instances,
    prefill_q,
    prefill_kv,
    span_len,
    page_seg,
    page_dest,
    page_row,
    dec_q,
    dec_new,
    cache_kv,
    block_table,
    cache_len,
):
    _, span, heads, width = prefill_q.shape
    pages = page_seg.shape[1]
    _, rows, steps = dec_q.shape[:3]
    pool, page = cache_kv.shape[1], cache_kv.shape[3]
    pages_max = block_table.shape[1] // rows
    capacity = -(-2 * pages // instances)
    requests = pages - capacity + 1
    groups = width // LANES
    per_row = steps * groups * heads
    block = LANES
    sizes = (heads, page, pages, rows, steps, pages_max, requests)
    dest = page_dest.reshape(1, pages)
    slot_width = 32
    f32, bf16, i32 = jnp.float32, jnp.bfloat16, jnp.int32
    shape = jax.ShapeDtypeStruct

    queries = query_rows(dec_q[0])
    q_slots = exchange(queries, instances)
    per_slot = instances // len(q_slots)

    fresh = dec_new.reshape(-1, LANES)
    source_kv = prefill_kv.reshape(-1, LANES)
    cache = cache_kv.reshape(-1, LANES)
    ints = (page_seg, dest, page_row, span_len, block_table, cache_len)
    info, part, lse, keys, vals, own_q = pl.pallas_call(
        functools.partial(cache_kernel, sizes),
        out_shape=(
            shape((8, slot_width), i32),
            shape((rows * per_row, LANES), f32),
            shape((rows * per_row, LANES), f32),
            shape((span, heads * LANES), bf16),
            shape((span, heads * LANES), bf16),
            shape(queries.shape, bf16),
        ),
        in_specs=[HBM_SPEC] * 10,
        out_specs=(SMEM_SPEC,) + (VMEM_SPEC,) * 5,
        scratch_shapes=[pltpu.SMEM(x.shape, i32) for x in ints]
        + [
            pltpu.VMEM((-(-fresh.shape[0] // LANES) * LANES, LANES), bf16),
            pltpu.VMEM(cache.shape, bf16),
            pltpu.VMEM(source_kv.shape, bf16),
            pltpu.VMEM((span * heads, LANES), f32),
            pltpu.SemaphoreType.DMA((10,)),
        ],
        compiler_params=params(),
        name="cache",
    )(*ints, queries, fresh, cache, source_kv)
    q_slots = [own_q] + q_slots[1:] if per_slot == 1 else q_slots

    count = requests * per_row
    tall = count + -(-(3 * -(-count // LANES) + 2) // 16) * 16
    own, sent = pl.pallas_call(
        functools.partial(pages_kernel, sizes + (instances,), per_slot),
        out_shape=(shape((count, LANES), f32), shape((tall, LANES), bf16)),
        in_specs=[SMEM_SPEC] + [VMEM_SPEC] * (len(q_slots) + 2),
        out_specs=(VMEM_SPEC, VMEM_SPEC),
        scratch_shapes=[pltpu.VMEM((count, LANES), bf16)],
        compiler_params=params(),
        name="pages",
    )(info, *q_slots, keys, vals)
    sent_slots = exchange(sent, instances)

    q_rows = query_rows(prefill_q[0])
    tile_rows = block * groups * heads
    tiles = span // block
    whole = lambda i: (0, 0)
    prefill_out = pl.pallas_call(
        functools.partial(prefill_kernel, (heads, page, pages, block)),
        out_shape=shape(q_rows.shape, bf16),
        grid=(tiles,),
        in_specs=[SMEM_SPEC]
        + [
            pl.BlockSpec((tile_rows, LANES), lambda i: (i, 0)),
            pl.BlockSpec(keys.shape, whole),
            pl.BlockSpec(vals.shape, whole),
            pl.BlockSpec(memory_space=pl.ANY),
        ],
        out_specs=pl.BlockSpec((tile_rows, LANES), lambda i: (i, 0)),
        scratch_shapes=[pltpu.VMEM((page * groups * heads, block), i32)],
        compiler_params=params(),
        name="prefill",
    )(info, q_rows, keys, vals, own)

    dec_out = pl.pallas_call(
        functools.partial(join_kernel, (heads, rows, requests, instances), per_slot),
        out_shape=shape((rows * per_row, LANES), bf16),
        in_specs=[VMEM_SPEC] * (3 + len(sent_slots)),
        out_specs=VMEM_SPEC,
        scratch_shapes=[pltpu.VMEM((rows * per_row, LANES), f32)] * 3
        + [
            pltpu.VMEM((-(-2 * instances // 8) * 8, LANES), i32),
            pltpu.SMEM((-(-2 * instances // 8) * 8, LANES), i32),
            pltpu.SemaphoreType.DMA,
        ],
        compiler_params=params(),
        name="join",
    )(own, *sent_slots, part, lse)

    return (
        from_rows(prefill_out, prefill_q.shape),
        from_rows(dec_out, dec_q.shape),
    )


def solution(mesh):
    return jax.shard_map(
        functools.partial(shards, mesh.shape["inst"]),
        mesh=mesh,
        in_specs=(
            P(("pool", "inst"), None, "tp", None),
            P(("pool", "inst"), None, None, "tp", None),
            P(("pool", "inst")),
            P(("pool", "inst"), None),
            P(("pool", "inst"), None, None),
            P(("pool", "inst"), None),
            P(("pool", "inst"), None, None, "tp", None),
            P(("pool", "inst"), None, None, None, "tp", None),
            P(("pool", "inst"), None, None, None, "tp", None),
            P(("pool", "inst"), None),
            P(("pool", "inst"), None),
        ),
        out_specs=(
            P(("pool", "inst"), None, "tp", None),
            P(("pool", "inst"), None, None, "tp", None),
        ),
        check_vma=False,
    )
```

```python
import functools
import math

import jax
import jax.numpy as jnp
from jax import lax
from jax.experimental import pallas as pl
from jax.experimental.pallas import tpu as pltpu
from jax.sharding import PartitionSpec as P

NEGATIVE = -1e30
LOG2E = math.log2(math.e)
LANES = 128
DIRECT = 8
VMEM_LIMIT = 48 * 1024 * 1024

SMEM_SPEC = pl.BlockSpec(memory_space=pltpu.SMEM)
HBM_SPEC = pl.BlockSpec(memory_space=pltpu.HBM)
VMEM_SPEC = pl.BlockSpec(memory_space=pltpu.VMEM)


def query_rows(field):
    lead = math.prod(field.shape[:-2])
    heads, width = field.shape[-2:]
    split = field.reshape(lead, heads, width // LANES, LANES)
    return split.transpose(0, 2, 1, 3).reshape(-1, LANES)


def from_rows(rows, shape):
    heads, width = shape[-2:]
    lead = math.prod(shape[:-2])
    split = rows.reshape(lead, width // LANES, heads, LANES)
    return split.transpose(0, 2, 1, 3).reshape(shape)


def head_of(shape, axis, heads):
    return lax.broadcasted_iota(jnp.int32, shape, axis) % heads


def dot_nt(first, second):
    return lax.dot_general(
        first, second, (((1,), (1,)), ((), ())), preferred_element_type=jnp.float32
    )


def dot_nn(first, second):
    return jnp.dot(first, second, preferred_element_type=jnp.float32)


def two_terms(weights):
    upper = weights.astype(jnp.bfloat16)
    lower = (weights - upper.astype(jnp.float32)).astype(jnp.bfloat16)
    return jnp.concatenate([upper, lower], axis=0)


def spread_heads(rows, heads):
    if heads == 1:
        return rows
    owner = head_of((16, LANES), 0, heads)
    tall = rows.reshape(-1, 16, LANES)
    parts = []
    for h in range(heads):
        mark = jnp.where(owner == h, 1.0, 0.0).astype(rows.dtype)
        parts.append((tall * mark[None]).reshape(rows.shape))
    return jnp.concatenate(parts, axis=1)


def pick_head(wide, heads):
    if heads == 1:
        return wide
    owner = head_of((wide.shape[0], LANES), 0, heads)
    picked = wide[:, :LANES]
    for h in range(1, heads):
        picked = jnp.where(owner == h, wide[:, h * LANES : (h + 1) * LANES], picked)
    return picked


def cache_kernel(
    sizes, len_ref, seg_hbm, dest_hbm, row_hbm, table_hbm, clen_hbm,
    q_hbm, fresh_hbm, pool_hbm, kv_hbm,
    info_ref, part_ref, lse_ref, keys_ref, vals_ref, own_q_ref,
    seg_ref, dest_ref, row_ref, table_ref, clen_ref,
    fresh_ref, pool_ref, kv_ref, scr_ref, sems,
):
    heads, page, pages, rows, steps, pages_max, requests = sizes
    copies = [
        pltpu.make_async_copy(source, target, sems.at[i])
        for i, (source, target) in enumerate((
            (seg_hbm, seg_ref), (dest_hbm, dest_ref), (row_hbm, row_ref),
            (kv_hbm, kv_ref), (table_hbm, table_ref), (clen_hbm, clen_ref),
            (q_hbm, own_q_ref), (fresh_hbm, fresh_ref.at[: fresh_hbm.shape[0]]),
            (pool_hbm, pool_ref),
        ))
    ]
    if fresh_ref.shape[0] > fresh_hbm.shape[0]:
        fresh_ref[fresh_hbm.shape[0] :, :] = jnp.zeros(
            (fresh_ref.shape[0] - fresh_hbm.shape[0], LANES), fresh_ref.dtype
        )
    for copy in copies:
        copy.start()
    span = pages * page

    for r in range(info_ref.shape[1]):
        info_ref[0, r] = 0
        info_ref[1, r] = 0
        info_ref[2, r] = -1
        info_ref[3, r] = 0
    for copy in copies[:3]:
        copy.wait()
    length = len_ref[0]
    info_ref[5, 0] = length

    def note(p, _):
        r = seg_ref[0, p]
        fresh_request = jnp.logical_or(p == 0, r != seg_ref[0, jnp.maximum(p - 1, 0)])

        @pl.when(fresh_request)
        def _():
            info_ref[0, r] = p * page
            info_ref[2, r] = jnp.where(p * page < length, dest_ref[0, p], -1)
            info_ref[3, r] = row_ref[0, p]

        info_ref[1, r] = jnp.minimum((p + 1) * page, length)
        info_ref[4, p] = info_ref[0, r]
        return 0

    lax.fori_loop(0, pages, note, 0)

    copies[3].wait()
    for part, out_ref in enumerate((keys_ref, vals_ref)):
        if heads == 1:
            out_ref[...] = kv_ref[part * span : (part + 1) * span, :]
        else:
            scr_ref[...] = kv_ref[part * span * heads : (part + 1) * span * heads, :].astype(
                jnp.float32
            )
            for h in range(heads):
                out_ref[:, h * LANES : (h + 1) * LANES] = scr_ref[
                    pl.ds(h, span, stride=heads), :
                ].astype(jnp.bfloat16)

    for copy in copies[4:]:
        copy.wait()
    scale2 = LANES**-0.5 * LOG2E
    per_row = own_q_ref.shape[0] // rows
    groups = per_row // (steps * heads)
    fresh = fresh_ref[...]
    width = fresh.shape[0]
    page_rows = page * heads

    col = lax.broadcasted_iota(jnp.int32, (per_row, width), 1)
    sub = lax.broadcasted_iota(jnp.int32, (per_row, width), 0)
    fresh_ok = (
        ((col // heads) % 2 == 0)
        & ((col // (2 * heads)) % steps <= sub // (groups * heads))
        & (col % heads == sub % heads)
    )
    fresh_row = jnp.where(fresh_ok, col // (2 * heads * steps), -1)
    ccol = lax.broadcasted_iota(jnp.int32, (per_row, pages_max * page_rows), 1)
    csub = lax.broadcasted_iota(jnp.int32, (per_row, pages_max * page_rows), 0)
    far = rows * pages_max * page
    token = jnp.where(ccol % heads == csub % heads, ccol // heads, far)

    def gather(b, part):
        pieces = []
        for j in range(pages_max):
            spot = (table_ref[0, b * pages_max + j] * 2 + part) * page_rows
            pieces.append(pool_ref[pl.ds(pl.multiple_of(spot, page_rows), page_rows), :])
        return jnp.concatenate(pieces, axis=0)

    def row_slice(b):
        return slice(b * per_row, (b + 1) * per_row)

    fresh_scores = [dot_nt(own_q_ref[row_slice(b), :], fresh) for b in range(rows)]
    scores = [dot_nt(own_q_ref[row_slice(b), :], gather(b, 0)) for b in range(rows)]
    cache_terms, fresh_terms, totals = [], [], []
    for b in range(rows):
        s_c = jnp.where(token < clen_ref[0, b], scores[b], NEGATIVE)
        s_f = jnp.where(fresh_row == b, fresh_scores[b], NEGATIVE)
        pieces = [s_c[:, i : i + width] for i in range(0, s_c.shape[1], width)] + [s_f]
        top = functools.reduce(jnp.maximum, pieces)
        top = jnp.max(top, axis=1, keepdims=True)
        weights = [jnp.exp2((piece - top) * scale2) for piece in pieces]
        total = jnp.sum(functools.reduce(jnp.add, weights), axis=1, keepdims=True)
        cache_terms.append(two_terms(jnp.concatenate(weights[:-1], axis=1)))
        fresh_terms.append(pltpu.roll(weights[-1], heads, 1))
        totals.append(total)
        lse = top * scale2 + jnp.log2(total)
        lse_ref[row_slice(b), :] = jnp.broadcast_to(lse, (per_row, LANES))
    count = rows * per_row
    fresh_acc = dot_nn(two_terms(jnp.concatenate(fresh_terms, axis=0)), fresh)
    fresh_acc = fresh_acc[:count] + fresh_acc[count:]
    for b in range(rows):
        acc = dot_nn(cache_terms[b], gather(b, 1))
        acc = acc[:per_row] + acc[per_row:] + fresh_acc[row_slice(b)]
        part_ref[row_slice(b), :] = acc * (1.0 / totals[b])


def pages_kernel(sizes, per_slot, info_ref, *refs):
    heads, page, pages, rows, steps, pages_max, requests, instances = sizes
    slot_count = instances // per_slot
    slots = refs[:slot_count]
    keys_ref, vals_ref, own_ref, send_ref, q_scr = refs[slot_count:]
    me = lax.axis_index("inst")
    per_row = slots[0].shape[0] // (per_slot * rows)
    span = pages * page
    scale2 = LANES**-0.5 * LOG2E
    for r in range(requests):
        slot = lax.rem(me - info_ref[2, r] + instances, instances)
        row = info_ref[3, r]
        if slot_count == 1:
            start = pl.multiple_of((slot * rows + row) * per_row, per_row)
            q_scr[r * per_row : (r + 1) * per_row, :] = slots[0][pl.ds(start, per_row), :]
        else:
            start = pl.multiple_of(row * per_row, per_row)
            for k in range(slot_count):

                @pl.when(slot == k)
                def _():
                    q_scr[r * per_row : (r + 1) * per_row, :] = slots[k][pl.ds(start, per_row), :]

    scores = dot_nt(spread_heads(q_scr[...], heads), keys_ref[...])
    token = lax.broadcasted_iota(jnp.int32, (per_row, span), 1)
    weights, tops, totals = [], [], []
    for r in range(requests):
        keep = (token >= info_ref[0, r]) & (token < info_ref[1, r])
        s_r = jnp.where(keep, scores[r * per_row : (r + 1) * per_row], NEGATIVE)
        top = jnp.max(s_r, axis=1, keepdims=True)
        w_r = jnp.where(keep, jnp.exp2((s_r - top) * scale2), 0.0)
        weights.append(w_r)
        tops.append(top)
        totals.append(jnp.sum(w_r, axis=1, keepdims=True))
    count = requests * per_row
    acc = dot_nn(two_terms(jnp.concatenate(weights, axis=0)), vals_ref[...])
    acc = pick_head(acc[:count] + acc[count:], heads)
    total = jnp.concatenate(totals, axis=0)
    live = total > 0.0
    blended = jnp.where(live, acc / jnp.where(live, total, 1.0), 0.0)
    lse = jnp.where(
        live,
        jnp.concatenate(tops, axis=0) * scale2 + jnp.log2(jnp.where(live, total, 1.0)),
        NEGATIVE,
    )
    own_ref[...] = blended
    send_ref[:count, :] = blended.astype(jnp.bfloat16)
    blocks = -(-count // LANES)
    lines = []
    for j in range(blocks):
        piece = lse[j * LANES : min((j + 1) * LANES, count)]
        shape = (piece.shape[0], LANES)
        same = lax.broadcasted_iota(jnp.int32, shape, 0) == lax.broadcasted_iota(
            jnp.int32, shape, 1
        )
        lines.append(jnp.sum(jnp.where(same, piece, 0.0), axis=0, keepdims=True))
    line = jnp.concatenate(lines, axis=0)
    first = line.astype(jnp.bfloat16)
    rest = line - first.astype(jnp.float32)
    second = rest.astype(jnp.bfloat16)
    third = (rest - second.astype(jnp.float32)).astype(jnp.bfloat16)
    terms = [t.astype(jnp.float32) for t in (first, second, third)]
    lane = lax.broadcasted_iota(jnp.int32, (1, LANES), 1)
    for f in (2, 3):
        tags = jnp.full((1, LANES), -1, jnp.int32)
        for r in range(requests):
            tags = jnp.where(lane == r, info_ref[f, r], tags)
        terms.append(tags.astype(jnp.float32))
    spare = send_ref.shape[0] - count
    terms.append(jnp.zeros((spare - 3 * blocks - 2, LANES), jnp.float32))
    send_ref[count:, :] = jnp.concatenate(terms, axis=0).astype(jnp.bfloat16)


def prefill_kernel(sizes, info_ref, q_ref, keys_ref, vals_ref, after_ref, out_ref, lag_ref):
    heads, page, pages, block = sizes
    tile = pl.program_id(0)
    page_rows = out_ref.shape[0] * page // block
    per_token = page_rows // page
    per_block = block // page
    scale2 = LANES**-0.5 * LOG2E
    length = info_ref[5, 0]

    @pl.when(tile == 0)
    def _():
        lane = lax.broadcasted_iota(jnp.int32, lag_ref.shape, 1)
        lag_ref[...] = lane - lax.broadcasted_iota(jnp.int32, lag_ref.shape, 0) // per_token

    first_key = info_ref[4, tile * per_block]
    first_block = first_key // block
    behind = tile - first_block

    def attend(count):
        base = (tile - (count - 1)) * block
        keys = keys_ref[pl.ds(pl.multiple_of(base, block), count * block), :]
        vals = vals_ref[pl.ds(pl.multiple_of(base, block), count * block), :]
        lane = lax.broadcasted_iota(jnp.int32, (1, block), 1)
        def score(p):
            rows = slice(p * page_rows, (p + 1) * page_rows)
            return dot_nt(spread_heads(q_ref[rows, :], heads), keys)

        ahead = score(0)
        for p in range(per_block):
            rows = slice(p * page_rows, (p + 1) * page_rows)
            scores = ahead
            if p + 1 < per_block:
                ahead = score(p + 1)
            start = info_ref[4, tile * per_block + p] - base
            pieces = []
            for j in range(count):
                s_j = scores[:, j * block : (j + 1) * block]
                keep = lane >= start - j * block
                if j == count - 1:
                    keep = keep & (lag_ref[...] <= p * page)
                pieces.append(jnp.where(keep, s_j, NEGATIVE))
            top = pieces[0]
            for piece in pieces[1:]:
                top = jnp.maximum(top, piece)
            top = jnp.max(top, axis=1, keepdims=True)
            weights = [jnp.exp2((piece - top) * scale2) for piece in pieces]
            total = weights[0]
            for w_j in weights[1:]:
                total = total + w_j
            total = jnp.sum(total, axis=1, keepdims=True)
            joined = jnp.concatenate([w_j.astype(jnp.bfloat16) for w_j in weights], axis=1)
            acc = pick_head(dot_nn(joined, vals), heads)
            place = lax.broadcasted_iota(jnp.int32, (page_rows, 1), 0) // per_token
            live = place < length - (tile * block + p * page)
            out_ref[rows, :] = (acc * jnp.where(live, 1.0 / total, 0.0)).astype(jnp.bfloat16)

    longest = 3
    for count in range(1, longest + 1):
        pl.when(behind == count - 1)(functools.partial(attend, count))


def join_kernel(sizes, per_slot, *refs):
    heads, rows, requests, instances = sizes
    slot_count = instances // per_slot
    own_ref = refs[0]
    sent = refs[1 : slot_count + 1]
    part_ref, lse_ref, out_ref, top_scr, total_scr, acc_scr, tag_scr, tags, sem = refs[slot_count + 1 :]
    me = lax.axis_index("inst")
    per_row = part_ref.shape[0] // rows
    count = requests * per_row
    blocks = -(-count // LANES)
    tall = sent[0].shape[0] // per_slot
    lines = []
    for n in range(instances):
        k, i = divmod(n, per_slot)
        stats = sent[k][i * tall + count : (i + 1) * tall, :].astype(jnp.float32)
        lines.append(
            stats[:blocks] + stats[blocks : 2 * blocks] + stats[2 * blocks : 3 * blocks]
        )
        tag_scr[n : n + 1, :] = stats[3 * blocks : 3 * blocks + 1].astype(jnp.int32)
        tag_scr[instances + n : instances + n + 1, :] = stats[
            3 * blocks + 1 : 3 * blocks + 2
        ].astype(jnp.int32)
    copy = pltpu.make_async_copy(tag_scr, tags, sem)
    copy.start()
    top_scr[...] = lse_ref[...]
    total_scr[...] = jnp.ones_like(total_scr)
    acc_scr[...] = part_ref[...]
    lane = lax.broadcasted_iota(jnp.int32, (per_row, LANES), 1)
    sub = lax.broadcasted_iota(jnp.int32, (per_row, LANES), 0)
    copy.wait()
    for n in range(instances):
        k, i = divmod(n, per_slot)
        for r in range(requests):

            @pl.when(tags[n, r] == me)
            def _():
                start = pl.multiple_of(tags[instances + n, r] * per_row, per_row)
                place = pl.ds(start, per_row)
                j, offset = divmod(r * per_row, LANES)
                spread = jnp.where(lane == sub + offset, lines[n][j : j + 1, :], 0.0)
                level = jnp.sum(spread, axis=1, keepdims=True)
                spot = r * per_row
                if n == 0:
                    values = own_ref[spot : spot + per_row, :]
                else:
                    spot = spot + i * tall
                    values = sent[k][spot : spot + per_row, :].astype(jnp.float32)
                top = top_scr[place, :]
                joined = jnp.maximum(top, level)
                old = jnp.exp2(top - joined)
                new = jnp.exp2(level - joined)
                top_scr[place, :] = joined
                total_scr[place, :] = total_scr[place, :] * old + new
                acc_scr[place, :] = acc_scr[place, :] * old + values * new

    out_ref[...] = (acc_scr[...] / total_scr[...]).astype(jnp.bfloat16)


def exchange(block, instances):
    if instances <= DIRECT:
        slots = [block]
        for k in range(1, instances):
            slots.append(
                lax.ppermute(block, "inst", [(i, (i + k) % instances) for i in range(instances)])
            )
        return slots
    whole = lax.all_gather(block, "inst", axis=0)
    order = lax.rem(lax.axis_index("inst") - jnp.arange(instances) + instances, instances)
    return [jnp.take(whole, order, axis=0).reshape((-1,) + block.shape[1:])]


def in_hbm(field):
    return pltpu.with_memory_space_constraint(field, pltpu.HBM)


def params(**extra):
    return pltpu.CompilerParams(vmem_limit_bytes=VMEM_LIMIT, **extra)


def shards(
    instances,
    prefill_q,
    prefill_kv,
    span_len,
    page_seg,
    page_dest,
    page_row,
    dec_q,
    dec_new,
    cache_kv,
    block_table,
    cache_len,
):
    _, span, heads, width = prefill_q.shape
    pages = page_seg.shape[1]
    _, rows, steps = dec_q.shape[:3]
    pool, page = cache_kv.shape[1], cache_kv.shape[3]
    pages_max = block_table.shape[1] // rows
    capacity = -(-2 * pages // instances)
    requests = pages - capacity + 1
    groups = width // LANES
    per_row = steps * groups * heads
    block = LANES
    sizes = (heads, page, pages, rows, steps, pages_max, requests)
    dest = page_dest.reshape(1, pages)
    slot_width = 32
    f32, bf16, i32 = jnp.float32, jnp.bfloat16, jnp.int32
    shape = jax.ShapeDtypeStruct

    queries = query_rows(dec_q[0])
    q_slots = exchange(queries, instances)
    per_slot = instances // len(q_slots)

    fresh = dec_new.reshape(-1, LANES)
    source_kv = prefill_kv.reshape(-1, LANES)
    cache = cache_kv.reshape(-1, LANES)
    ints = (page_seg, dest, page_row, block_table, cache_len)
    info, part, lse, keys, vals, own_q = pl.pallas_call(
        functools.partial(cache_kernel, sizes),
        out_shape=(
            shape((8, slot_width), i32),
            shape((rows * per_row, LANES), f32),
            shape((rows * per_row, LANES), f32),
            shape((span, heads * LANES), bf16),
            shape((span, heads * LANES), bf16),
            shape(queries.shape, bf16),
        ),
        in_specs=[SMEM_SPEC] + [HBM_SPEC] * 9,
        out_specs=(SMEM_SPEC,) + (VMEM_SPEC,) * 5,
        scratch_shapes=[pltpu.SMEM(x.shape, i32) for x in ints]
        + [
            pltpu.VMEM((-(-fresh.shape[0] // LANES) * LANES, LANES), bf16),
            pltpu.VMEM(cache.shape, bf16),
            pltpu.VMEM(source_kv.shape, bf16),
            pltpu.VMEM((span * heads, LANES), f32),
            pltpu.SemaphoreType.DMA((9,)),
        ],
        compiler_params=params(),
        name="cache",
    )(span_len, *map(in_hbm, (*ints, queries, fresh, cache, source_kv)))
    q_slots = [own_q] + q_slots[1:] if per_slot == 1 else q_slots

    count = requests * per_row
    tall = count + -(-(3 * -(-count // LANES) + 2) // 16) * 16
    own, sent = pl.pallas_call(
        functools.partial(pages_kernel, sizes + (instances,), per_slot),
        out_shape=(shape((count, LANES), f32), shape((tall, LANES), bf16)),
        in_specs=[SMEM_SPEC] + [VMEM_SPEC] * (len(q_slots) + 2),
        out_specs=(VMEM_SPEC, VMEM_SPEC),
        scratch_shapes=[pltpu.VMEM((count, LANES), bf16)],
        compiler_params=params(),
        name="pages",
    )(info, *q_slots, keys, vals)
    sent_slots = exchange(sent, instances)

    q_rows = query_rows(prefill_q[0])
    tile_rows = block * groups * heads
    tiles = span // block
    whole = lambda i: (0, 0)
    prefill_out = pl.pallas_call(
        functools.partial(prefill_kernel, (heads, page, pages, block)),
        out_shape=shape(q_rows.shape, bf16),
        grid=(tiles,),
        in_specs=[SMEM_SPEC]
        + [
            pl.BlockSpec((tile_rows, LANES), lambda i: (i, 0)),
            pl.BlockSpec(keys.shape, whole),
            pl.BlockSpec(vals.shape, whole),
            pl.BlockSpec(memory_space=pl.ANY),
        ],
        out_specs=pl.BlockSpec((tile_rows, LANES), lambda i: (i, 0)),
        scratch_shapes=[pltpu.VMEM((page * groups * heads, block), i32)],
        compiler_params=params(),
        name="prefill",
    )(info, q_rows, keys, vals, own)

    dec_out = pl.pallas_call(
        functools.partial(join_kernel, (heads, rows, requests, instances), per_slot),
        out_shape=shape((rows * per_row, LANES), bf16),
        in_specs=[VMEM_SPEC] * (3 + len(sent_slots)),
        out_specs=VMEM_SPEC,
        scratch_shapes=[pltpu.VMEM((rows * per_row, LANES), f32)] * 3
        + [
            pltpu.VMEM((-(-2 * instances // 8) * 8, LANES), i32),
            pltpu.SMEM((-(-2 * instances // 8) * 8, LANES), i32),
            pltpu.SemaphoreType.DMA,
        ],
        compiler_params=params(),
        name="join",
    )(own, *sent_slots, part, lse)

    return (
        from_rows(prefill_out, prefill_q.shape),
        from_rows(dec_out, dec_q.shape),
    )


def solution(mesh):
    return jax.shard_map(
        functools.partial(shards, mesh.shape["inst"]),
        mesh=mesh,
        in_specs=(
            P(("pool", "inst"), None, "tp", None),
            P(("pool", "inst"), None, None, "tp", None),
            P(("pool", "inst")),
            P(("pool", "inst"), None),
            P(("pool", "inst"), None, None),
            P(("pool", "inst"), None),
            P(("pool", "inst"), None, None, "tp", None),
            P(("pool", "inst"), None, None, None, "tp", None),
            P(("pool", "inst"), None, None, None, "tp", None),
            P(("pool", "inst"), None),
            P(("pool", "inst"), None),
        ),
        out_specs=(
            P(("pool", "inst"), None, "tp", None),
            P(("pool", "inst"), None, None, "tp", None),
        ),
        check_vma=False,
    )
```

```python
import functools
import math

import jax
import jax.numpy as jnp
from jax import lax
from jax.experimental import pallas as pl
from jax.experimental.pallas import tpu as pltpu
from jax.sharding import PartitionSpec as P

NEGATIVE = -1e30
LOG2E = math.log2(math.e)
LANES = 128
DIRECT = 8
EARLY = 2
VMEM_LIMIT = 48 * 1024 * 1024

SMEM_SPEC = pl.BlockSpec(memory_space=pltpu.SMEM)
BRIEF = pl.CostEstimate(flops=1000, bytes_accessed=1000, transcendentals=0)
ANY_SPEC = pl.BlockSpec(memory_space=pl.ANY)
HBM_SPEC = pl.BlockSpec(memory_space=pltpu.HBM)
VMEM_SPEC = pl.BlockSpec(memory_space=pltpu.VMEM)


def query_rows(field):
    lead = math.prod(field.shape[:-2])
    heads, width = field.shape[-2:]
    split = field.reshape(lead, heads, width // LANES, LANES)
    return split.transpose(0, 2, 1, 3).reshape(-1, LANES)


def from_rows(rows, shape):
    heads, width = shape[-2:]
    lead = math.prod(shape[:-2])
    split = rows.reshape(lead, width // LANES, heads, LANES)
    return split.transpose(0, 2, 1, 3).reshape(shape)


def head_of(shape, axis, heads):
    return lax.broadcasted_iota(jnp.int32, shape, axis) % heads


def dot_nt(first, second):
    return lax.dot_general(
        first, second, (((1,), (1,)), ((), ())), preferred_element_type=jnp.float32
    )


def dot_nn(first, second):
    return jnp.dot(first, second, preferred_element_type=jnp.float32)


def two_terms(weights):
    upper = weights.astype(jnp.bfloat16)
    lower = (weights - upper.astype(jnp.float32)).astype(jnp.bfloat16)
    return jnp.concatenate([upper, lower], axis=0)


def spread_heads(rows, heads):
    if heads == 1:
        return rows
    owner = head_of((16, LANES), 0, heads)
    tall = rows.reshape(-1, 16, LANES)
    parts = []
    for h in range(heads):
        mark = jnp.where(owner == h, 1.0, 0.0).astype(rows.dtype)
        parts.append((tall * mark[None]).reshape(rows.shape))
    return jnp.concatenate(parts, axis=1)


def pick_head(wide, heads):
    if heads == 1:
        return wide
    owner = head_of((wide.shape[0], LANES), 0, heads)
    picked = wide[:, :LANES]
    for h in range(1, heads):
        picked = jnp.where(owner == h, wide[:, h * LANES : (h + 1) * LANES], picked)
    return picked


def cache_kernel(
    sizes, len_ref, seg_hbm, dest_hbm, row_hbm, table_hbm, clen_hbm,
    q_hbm, fresh_hbm, pool_hbm, kv_hbm,
    info_ref, lse_ref, total_ref, part_ref, keys_ref, vals_ref, own_q_ref,
    seg_ref, dest_ref, row_ref, table_ref, clen_ref,
    fresh_ref, pool_ref, kv_ref, scr_ref, sems,
):
    heads, page, pages, rows, steps, pages_max, requests = sizes
    copies = [
        pltpu.make_async_copy(source, target, sems.at[i])
        for i, (source, target) in enumerate((
            (seg_hbm, seg_ref), (dest_hbm, dest_ref), (row_hbm, row_ref),
            (kv_hbm, kv_ref), (table_hbm, table_ref), (clen_hbm, clen_ref),
            (q_hbm, own_q_ref), (fresh_hbm, fresh_ref.at[: fresh_hbm.shape[0]]),
            (pool_hbm, pool_ref),
        ))
    ]
    if fresh_ref.shape[0] > fresh_hbm.shape[0]:
        fresh_ref[fresh_hbm.shape[0] :, :] = jnp.zeros(
            (fresh_ref.shape[0] - fresh_hbm.shape[0], LANES), fresh_ref.dtype
        )
    for copy in copies:
        copy.start()
    total_ref[...] = jnp.ones_like(total_ref)
    span = pages * page

    for r in range(requests):
        info_ref[0, r] = 0
        info_ref[1, r] = 0
        info_ref[2, r] = -1
        info_ref[3, r] = 0
    for copy in copies[:3]:
        copy.wait()
    length = len_ref[0]
    info_ref[5, 0] = length
    for p in reversed(range(pages)):
        r = seg_ref[0, p]
        info_ref[0, r] = p * page
        info_ref[2, r] = jnp.where(p * page < length, dest_ref[0, p], -1)
        info_ref[3, r] = row_ref[0, p]
    for p in range(pages):
        r = seg_ref[0, p]
        info_ref[1, r] = jnp.minimum((p + 1) * page, length)
        info_ref[4, p] = info_ref[0, r]

    copies[3].wait()
    for part, out_ref in enumerate((keys_ref, vals_ref)):
        if heads == 1:
            out_ref[...] = kv_ref[part * span : (part + 1) * span, :]
        else:
            scr_ref[...] = kv_ref[part * span * heads : (part + 1) * span * heads, :].astype(
                jnp.float32
            )
            for h in range(heads):
                out_ref[:, h * LANES : (h + 1) * LANES] = scr_ref[
                    pl.ds(h, span, stride=heads), :
                ].astype(jnp.bfloat16)

    for copy in copies[4:]:
        copy.wait()
    scale2 = LANES**-0.5 * LOG2E
    per_row = own_q_ref.shape[0] // rows
    groups = per_row // (steps * heads)
    fresh = fresh_ref[...]
    width = fresh.shape[0]
    page_rows = page * heads

    col = lax.broadcasted_iota(jnp.int32, (per_row, width), 1)
    sub = lax.broadcasted_iota(jnp.int32, (per_row, width), 0)
    fresh_ok = (
        ((col // heads) % 2 == 0)
        & ((col // (2 * heads)) % steps <= sub // (groups * heads))
        & (col % heads == sub % heads)
    )
    fresh_row = jnp.where(fresh_ok, col // (2 * heads * steps), -1)
    ccol = lax.broadcasted_iota(jnp.int32, (per_row, pages_max * page_rows), 1)
    csub = lax.broadcasted_iota(jnp.int32, (per_row, pages_max * page_rows), 0)
    far = rows * pages_max * page
    token = jnp.where(ccol % heads == csub % heads, ccol // heads, far)

    def gather(b, part):
        pieces = []
        for j in range(pages_max):
            spot = (table_ref[0, b * pages_max + j] * 2 + part) * page_rows
            pieces.append(pool_ref[pl.ds(pl.multiple_of(spot, page_rows), page_rows), :])
        return jnp.concatenate(pieces, axis=0)

    def row_slice(b):
        return slice(b * per_row, (b + 1) * per_row)

    fresh_scores = [dot_nt(own_q_ref[row_slice(b), :], fresh) for b in range(rows)]
    scores = [dot_nt(own_q_ref[row_slice(b), :], gather(b, 0)) for b in range(rows)]
    cache_terms, fresh_terms, totals = [], [], []
    for b in range(rows):
        s_c = jnp.where(token < clen_ref[0, b], scores[b], NEGATIVE)
        s_f = jnp.where(fresh_row == b, fresh_scores[b], NEGATIVE)
        pieces = [s_c[:, i : i + width] for i in range(0, s_c.shape[1], width)] + [s_f]
        top = functools.reduce(jnp.maximum, pieces)
        top = jnp.max(top, axis=1, keepdims=True)
        weights = [jnp.exp2((piece - top) * scale2) for piece in pieces]
        total = jnp.sum(functools.reduce(jnp.add, weights), axis=1, keepdims=True)
        cache_terms.append(two_terms(jnp.concatenate(weights[:-1], axis=1)))
        fresh_terms.append(pltpu.roll(weights[-1], heads, 1))
        totals.append(total)
        lse = top * scale2 + jnp.log2(total)
        lse_ref[row_slice(b), :] = jnp.broadcast_to(lse, (per_row, LANES))
    count = rows * per_row
    fresh_acc = dot_nn(two_terms(jnp.concatenate(fresh_terms, axis=0)), fresh)
    fresh_acc = fresh_acc[:count] + fresh_acc[count:]
    for b in range(rows):
        acc = dot_nn(cache_terms[b], gather(b, 1))
        acc = acc[:per_row] + acc[per_row:] + fresh_acc[row_slice(b)]
        part_ref[row_slice(b), :] = acc * (1.0 / totals[b])


def pages_kernel(sizes, partners, info_ref, *refs):
    heads, page, pages, rows, requests, capacity, instances = sizes
    slot_count = 1 if partners is None else len(partners)
    slots = refs[:slot_count]
    keys_ref, vals_ref, _, own_ref, send_ref, token_ref, q_scr = refs[slot_count:]
    me = lax.axis_index("inst")
    span = pages * page
    scale2 = LANES**-0.5 * LOG2E
    count = own_ref.shape[0]
    per_row = count // requests
    token_ref[...] = jnp.zeros_like(token_ref)
    for r in range(requests):
        dest, row = info_ref[2, r], info_ref[3, r]
        place = slice(r * per_row, (r + 1) * per_row)
        if partners is None:
            start = pl.multiple_of((jnp.maximum(dest, 0) * rows + row) * per_row, per_row)
            q_scr[place, :] = slots[0][pl.ds(start, per_row), :]
        else:
            start = pl.multiple_of(row * per_row, per_row)
            picked = slots[0][pl.ds(start, per_row), :]
            for k, offset in enumerate(partners[1:]):
                other = slots[k + 1][pl.ds(start, per_row), :]
                picked = jnp.where(dest == jnp.bitwise_xor(me, offset), other, picked)
            q_scr[place, :] = picked

    cut = capacity * page
    totals, tops, accs = [], [], []
    for low, high, first, last in ((0, cut, 0, 1), (cut, span, 1, requests)):
        wide = high - low
        scores = dot_nt(
            spread_heads(q_scr[first * per_row : last * per_row, :], heads), keys_ref[low:high, :]
        )
        token = low + lax.broadcasted_iota(jnp.int32, (per_row, wide), 1)
        weights = []
        for r in range(first, last):
            keep = (token >= info_ref[0, r]) & (token < info_ref[1, r])
            spot = (r - first) * per_row
            s_r = jnp.where(keep, scores[spot : spot + per_row], NEGATIVE)
            top = jnp.max(s_r, axis=1, keepdims=True)
            w_r = jnp.where(keep, jnp.exp2((s_r - top) * scale2), 0.0)
            weights.append(w_r)
            tops.append(top)
            totals.append(jnp.sum(w_r, axis=1, keepdims=True))
        acc = dot_nn(two_terms(jnp.concatenate(weights, axis=0)), vals_ref[low:high, :])
        half = (last - first) * per_row
        accs.append(pick_head(acc[:half] + acc[half:], heads))
    acc = jnp.concatenate(accs, axis=0)
    total = jnp.concatenate(totals, axis=0)
    live = total > 0.0
    blended = jnp.where(live, acc / jnp.where(live, total, 1.0), 0.0)
    lse = jnp.where(
        live,
        jnp.concatenate(tops, axis=0) * scale2 + jnp.log2(jnp.where(live, total, 1.0)),
        NEGATIVE,
    )
    own_ref[...] = blended
    send_ref[:count, :] = blended.astype(jnp.bfloat16)
    blocks = -(-count // LANES)
    lines = []
    for j in range(blocks):
        piece = lse[j * LANES : min((j + 1) * LANES, count)]
        shape = (piece.shape[0], LANES)
        same = lax.broadcasted_iota(jnp.int32, shape, 0) == lax.broadcasted_iota(
            jnp.int32, shape, 1
        )
        lines.append(jnp.sum(jnp.where(same, piece, 0.0), axis=0, keepdims=True))
    line = jnp.concatenate(lines, axis=0)
    first = line.astype(jnp.bfloat16)
    rest = line - first.astype(jnp.float32)
    second = rest.astype(jnp.bfloat16)
    third = (rest - second.astype(jnp.float32)).astype(jnp.bfloat16)
    terms = [t.astype(jnp.float32) for t in (first, second, third)]
    lane = lax.broadcasted_iota(jnp.int32, (1, LANES), 1)
    for f in (2, 3):
        tags = jnp.full((1, LANES), -1, jnp.int32)
        for r in range(requests):
            tags = jnp.where(lane == r, info_ref[f, r], tags)
        terms.append(tags.astype(jnp.float32))
    spare = send_ref.shape[0] - count
    terms.append(jnp.zeros((spare - 3 * blocks - 2, LANES), jnp.float32))
    send_ref[count:, :] = jnp.concatenate(terms, axis=0).astype(jnp.bfloat16)


def prefill_kernel(sizes, first_tile, info_ref, q_ref, keys_ref, vals_ref, *refs):
    heads, page, pages, block = sizes
    out_ref, token_ref, lag_ref = refs[-3:]
    tile = pl.program_id(0) + first_tile
    token_ref[...] = jnp.zeros_like(token_ref)
    page_rows = out_ref.shape[0] * page // block
    per_token = page_rows // page
    per_block = block // page
    scale2 = LANES**-0.5 * LOG2E
    length = info_ref[5, 0]

    @pl.when(tile == first_tile)
    def _():
        lane = lax.broadcasted_iota(jnp.int32, lag_ref.shape, 1)
        lag_ref[...] = lane - lax.broadcasted_iota(jnp.int32, lag_ref.shape, 0) // per_token

    first_key = info_ref[4, tile * per_block]
    first_block = first_key // block
    behind = tile - first_block

    def attend(count):
        base = (tile - (count - 1)) * block
        keys = keys_ref[pl.ds(pl.multiple_of(base, block), count * block), :]
        vals = vals_ref[pl.ds(pl.multiple_of(base, block), count * block), :]
        lane = lax.broadcasted_iota(jnp.int32, (1, block), 1)
        def score(p):
            rows = slice(p * page_rows, (p + 1) * page_rows)
            return dot_nt(spread_heads(q_ref[rows, :], heads), keys)

        ahead = score(0)
        for p in range(per_block):
            rows = slice(p * page_rows, (p + 1) * page_rows)
            scores = ahead
            if p + 1 < per_block:
                ahead = score(p + 1)
            start = info_ref[4, tile * per_block + p] - base
            pieces = []
            for j in range(count):
                s_j = scores[:, j * block : (j + 1) * block]
                keep = lane >= start - j * block
                if j == count - 1:
                    keep = keep & (lag_ref[...] <= p * page)
                pieces.append(jnp.where(keep, s_j, NEGATIVE))
            top = pieces[0]
            for piece in pieces[1:]:
                top = jnp.maximum(top, piece)
            top = jnp.max(top, axis=1, keepdims=True)
            weights = [jnp.exp2((piece - top) * scale2) for piece in pieces]
            total = weights[0]
            for w_j in weights[1:]:
                total = total + w_j
            total = jnp.sum(total, axis=1, keepdims=True)
            joined = jnp.concatenate([w_j.astype(jnp.bfloat16) for w_j in weights], axis=1)
            acc = pick_head(dot_nn(joined, vals), heads)
            place = lax.broadcasted_iota(jnp.int32, (page_rows, 1), 0) // per_token
            live = place < length - (tile * block + p * page)
            out_ref[rows, :] = (acc * jnp.where(live, 1.0 / total, 0.0)).astype(jnp.bfloat16)

    longest = 3
    for count in range(1, longest + 1):
        pl.when(behind == count - 1)(functools.partial(attend, count))


def join_kernel(sizes, with_own, last, *refs):
    rows, requests, blocks_of = sizes
    sent_count = len(blocks_of)
    refs = list(refs)
    own_ref = refs.pop(0) if with_own else None
    sent, refs = refs[:sent_count], refs[sent_count:]
    top_in, total_in, acc_in = refs[:3]
    refs = refs[4:]
    if last:
        out_ref, top_scr, total_scr, acc_scr, tag_scr, tags, sem = refs
    else:
        top_scr, total_scr, acc_scr, token_ref, tag_scr, tags, sem = refs
        token_ref[...] = jnp.zeros_like(token_ref)
    me = lax.axis_index("inst")
    per_row = acc_in.shape[0] // rows
    count = requests * per_row
    blocks = -(-count // LANES)
    instances = sum(blocks_of)
    places = [(k, i) for k in range(sent_count) for i in range(blocks_of[k])]
    lines = []
    for n, (k, i) in enumerate(places):
        tall = sent[k].shape[0] // blocks_of[k]
        stats = sent[k][i * tall + count : (i + 1) * tall, :].astype(jnp.float32)
        lines.append(
            stats[:blocks] + stats[blocks : 2 * blocks] + stats[2 * blocks : 3 * blocks]
        )
        tag_scr[n : n + 1, :] = stats[3 * blocks : 3 * blocks + 1].astype(jnp.int32)
        tag_scr[instances + n : instances + n + 1, :] = stats[
            3 * blocks + 1 : 3 * blocks + 2
        ].astype(jnp.int32)
    copy = pltpu.make_async_copy(tag_scr, tags, sem)
    copy.start()
    top_scr[...] = top_in[...]
    total_scr[...] = total_in[...]
    acc_scr[...] = acc_in[...]
    lane = lax.broadcasted_iota(jnp.int32, (per_row, LANES), 1)
    sub = lax.broadcasted_iota(jnp.int32, (per_row, LANES), 0)
    copy.wait()
    for n, (k, i) in enumerate(places):
        tall = sent[k].shape[0] // blocks_of[k]
        for r in range(requests):

            @pl.when(tags[n, r] == me)
            def _():
                start = pl.multiple_of(tags[instances + n, r] * per_row, per_row)
                place = pl.ds(start, per_row)
                j, offset = divmod(r * per_row, LANES)
                spread = jnp.where(lane == sub + offset, lines[n][j : j + 1, :], 0.0)
                level = jnp.sum(spread, axis=1, keepdims=True)
                spot = r * per_row
                if with_own and n == 0:
                    values = own_ref[spot : spot + per_row, :]
                else:
                    spot = spot + i * tall
                    values = sent[k][spot : spot + per_row, :].astype(jnp.float32)
                top = top_scr[place, :]
                joined = jnp.maximum(top, level)
                old = jnp.exp2(top - joined)
                new = jnp.exp2(level - joined)
                top_scr[place, :] = joined
                total_scr[place, :] = total_scr[place, :] * old + new
                acc_scr[place, :] = acc_scr[place, :] * old + values * new

    if last:
        out_ref[...] = (acc_scr[...] / total_scr[...]).astype(jnp.bfloat16)


def swap(block, offset, instances):
    return lax.ppermute(block, "inst", [(i, i ^ offset) for i in range(instances)])


def gather_all(block):
    whole = lax.all_gather(block, "inst", axis=0)
    return whole.reshape((-1,) + block.shape[1:])


def in_hbm(field):
    return pltpu.with_memory_space_constraint(field, pltpu.HBM)


def params(**extra):
    return pltpu.CompilerParams(vmem_limit_bytes=VMEM_LIMIT, **extra)


def shards(
    instances,
    prefill_q,
    prefill_kv,
    span_len,
    page_seg,
    page_dest,
    page_row,
    dec_q,
    dec_new,
    cache_kv,
    block_table,
    cache_len,
):
    _, span, heads, width = prefill_q.shape
    pages = page_seg.shape[1]
    _, rows, steps = dec_q.shape[:3]
    pool, page = cache_kv.shape[1], cache_kv.shape[3]
    pages_max = block_table.shape[1] // rows
    capacity = -(-2 * pages // instances)
    requests = pages - capacity + 1
    groups = width // LANES
    per_row = steps * groups * heads
    block = LANES
    sizes = (heads, page, pages, rows, steps, pages_max, requests)
    dest = page_dest.reshape(1, pages)
    slot_width = 32
    f32, bf16, i32 = jnp.float32, jnp.bfloat16, jnp.int32
    shape = jax.ShapeDtypeStruct

    direct = instances <= DIRECT and instances & (instances - 1) == 0
    queries = query_rows(dec_q[0])
    if direct:
        arrived = {x: swap(queries, x, instances) for x in range(1, instances)}

    fresh = dec_new.reshape(-1, LANES)
    source_kv = prefill_kv.reshape(-1, LANES)
    cache = cache_kv.reshape(-1, LANES)
    ints = (page_seg, dest, page_row, block_table, cache_len)
    info, *state, keys, vals, own_q = pl.pallas_call(
        functools.partial(cache_kernel, sizes),
        out_shape=(
            shape((8, slot_width), i32),
            *[shape((rows * per_row, LANES), f32)] * 3,
            shape((span, heads * LANES), bf16),
            shape((span, heads * LANES), bf16),
            shape(queries.shape, bf16),
        ),
        in_specs=[SMEM_SPEC] + [HBM_SPEC] * 9,
        out_specs=(SMEM_SPEC,) + (VMEM_SPEC,) * 6,
        scratch_shapes=[pltpu.SMEM(x.shape, i32) for x in ints]
        + [
            pltpu.VMEM((-(-fresh.shape[0] // LANES) * LANES, LANES), bf16),
            pltpu.VMEM(cache.shape, bf16),
            pltpu.VMEM(source_kv.shape, bf16),
            pltpu.VMEM((span * heads, LANES), f32),
            pltpu.SemaphoreType.DMA((9,)),
        ],
        compiler_params=params(),
        cost_estimate=BRIEF,
        name="cache",
    )(span_len, *map(in_hbm, (*ints, queries, fresh, cache, source_kv)))
    count = requests * per_row
    tall = count + -(-(3 * -(-count // LANES) + 2) // 16) * 16
    token = shape((8, LANES), f32)

    def attend_pages(partners, slots, after):
        return pl.pallas_call(
            functools.partial(
                pages_kernel,
                (heads, page, pages, rows, requests, capacity, instances),
                partners,
            ),
            out_shape=(shape((count, LANES), f32), shape((tall, LANES), bf16), token),
            in_specs=[SMEM_SPEC] + [VMEM_SPEC] * (len(slots) + 2) + [ANY_SPEC],
            out_specs=(VMEM_SPEC,) * 3,
            scratch_shapes=[pltpu.VMEM((count, LANES), bf16)],
            compiler_params=params(),
            cost_estimate=BRIEF,
            name="pages",
        )(info, *slots, keys, vals, after)

    q_rows = query_rows(prefill_q[0])
    tile_rows = block * groups * heads
    tiles = span // block
    whole = lambda i: (0, 0)

    def attend_source(first, last, after, earlier=None):
        rest = [after] if earlier is None else [after, earlier]
        return pl.pallas_call(
            functools.partial(prefill_kernel, (heads, page, pages, block), first),
            out_shape=(shape(q_rows.shape, bf16), token),
            grid=(last - first,),
            in_specs=[SMEM_SPEC]
            + [
                pl.BlockSpec((tile_rows, LANES), lambda i: (i + first, 0)),
                pl.BlockSpec(keys.shape, whole),
                pl.BlockSpec(vals.shape, whole),
            ]
            + [ANY_SPEC] * len(rest),
            out_specs=(
                pl.BlockSpec((tile_rows, LANES), lambda i: (i + first, 0)),
                pl.BlockSpec(token.shape, whole),
            ),
            scratch_shapes=[pltpu.VMEM((page * groups * heads, block), i32)],
            input_output_aliases={} if earlier is None else {5: 0},
            compiler_params=params(),
            cost_estimate=BRIEF,
            name="prefill",
        )(info, q_rows, keys, vals, *rest)

    def join(own, sent, state, after, last):
        blocks_of = tuple(block.shape[0] // tall for block in sent)
        tag_rows = -(-2 * sum(blocks_of) // 8) * 8
        lead = [] if own is None else [own]
        whole_state = [shape((rows * per_row, LANES), f32)] * 3
        result = shape((rows * per_row, LANES), bf16)
        return pl.pallas_call(
            functools.partial(join_kernel, (rows, requests, blocks_of), own is not None, last),
            out_shape=result if last else (*whole_state, token),
            in_specs=[VMEM_SPEC] * (len(lead) + len(sent) + 3) + [ANY_SPEC],
            out_specs=VMEM_SPEC if last else (VMEM_SPEC,) * 4,
            scratch_shapes=[pltpu.VMEM(x.shape, f32) for x in whole_state if last]
            + [
                pltpu.VMEM((tag_rows, LANES), i32),
                pltpu.SMEM((tag_rows, LANES), i32),
                pltpu.SemaphoreType.DMA,
            ],
            compiler_params=params(),
            cost_estimate=BRIEF,
            name="join",
        )(*lead, *sent, *state, after)

    if direct and instances > 2:
        x, *near = range(instances - 1, 0, -1)
        own, block_own, done = attend_pages((0, x), [own_q, arrived[x]], state[0])
        far = swap(block_own, x, instances)
        prefill_out, done = attend_source(0, EARLY, done)
        _, sent, done = attend_pages(tuple(near), [arrived[x] for x in near], done)
        *state, done = join(own, [block_own, far], state, done, False)
        prefill_out, done = attend_source(EARLY, tiles, done, prefill_out)
        dec_out = join(None, [swap(sent, x, instances) for x in near], state, done, True)
    else:
        queries = gather_all(queries)
        own, sent, done = attend_pages(None, [queries], state[0])
        prefill_out, done = attend_source(0, tiles, done)
        dec_out = join(None, [gather_all(sent)], state, done, True)

    return (
        from_rows(prefill_out, prefill_q.shape),
        from_rows(dec_out, dec_q.shape),
    )


def solution(mesh):
    return jax.shard_map(
        functools.partial(shards, mesh.shape["inst"]),
        mesh=mesh,
        in_specs=(
            P(("pool", "inst"), None, "tp", None),
            P(("pool", "inst"), None, None, "tp", None),
            P(("pool", "inst")),
            P(("pool", "inst"), None),
            P(("pool", "inst"), None, None),
            P(("pool", "inst"), None),
            P(("pool", "inst"), None, None, "tp", None),
            P(("pool", "inst"), None, None, None, "tp", None),
            P(("pool", "inst"), None, None, None, "tp", None),
            P(("pool", "inst"), None),
            P(("pool", "inst"), None),
        ),
        out_specs=(
            P(("pool", "inst"), None, "tp", None),
            P(("pool", "inst"), None, None, "tp", None),
        ),
        check_vma=False,
    )
```

```python
import functools
import math

import jax
import jax.numpy as jnp
from jax import lax
from jax.experimental import pallas as pl
from jax.experimental.pallas import tpu as pltpu
from jax.sharding import PartitionSpec as P

NEGATIVE = -1e30
LOG2E = math.log2(math.e)
LANES = 128
DIRECT = 8
EARLY = 3
VMEM_LIMIT = 48 * 1024 * 1024

SMEM_SPEC = pl.BlockSpec(memory_space=pltpu.SMEM)
BRIEF = pl.CostEstimate(flops=1000, bytes_accessed=1000, transcendentals=0)
ANY_SPEC = pl.BlockSpec(memory_space=pl.ANY)
HBM_SPEC = pl.BlockSpec(memory_space=pltpu.HBM)
VMEM_SPEC = pl.BlockSpec(memory_space=pltpu.VMEM)


def query_rows(field):
    lead = math.prod(field.shape[:-2])
    heads, width = field.shape[-2:]
    split = field.reshape(lead, heads, width // LANES, LANES)
    return split.transpose(0, 2, 1, 3).reshape(-1, LANES)


def from_rows(rows, shape):
    heads, width = shape[-2:]
    lead = math.prod(shape[:-2])
    split = rows.reshape(lead, width // LANES, heads, LANES)
    return split.transpose(0, 2, 1, 3).reshape(shape)


def head_of(shape, axis, heads):
    return lax.broadcasted_iota(jnp.int32, shape, axis) % heads


def dot_nt(first, second):
    return lax.dot_general(
        first, second, (((1,), (1,)), ((), ())), preferred_element_type=jnp.float32
    )


def dot_nn(first, second):
    return jnp.dot(first, second, preferred_element_type=jnp.float32)


def two_terms(weights):
    upper = weights.astype(jnp.bfloat16)
    lower = (weights - upper.astype(jnp.float32)).astype(jnp.bfloat16)
    return jnp.concatenate([upper, lower], axis=0)


def spread_heads(rows, heads):
    if heads == 1:
        return rows
    owner = head_of((16, LANES), 0, heads)
    tall = rows.reshape(-1, 16, LANES)
    parts = []
    for h in range(heads):
        mark = jnp.where(owner == h, 1.0, 0.0).astype(rows.dtype)
        parts.append((tall * mark[None]).reshape(rows.shape))
    return jnp.concatenate(parts, axis=1)


def pick_head(wide, heads):
    if heads == 1:
        return wide
    owner = head_of((wide.shape[0], LANES), 0, heads)
    picked = wide[:, :LANES]
    for h in range(1, heads):
        picked = jnp.where(owner == h, wide[:, h * LANES : (h + 1) * LANES], picked)
    return picked


def cache_kernel(
    sizes, len_ref, seg_hbm, dest_hbm, row_hbm, table_hbm, clen_hbm,
    q_hbm, fresh_hbm, pool_hbm, kv_hbm,
    info_ref, lse_ref, total_ref, part_ref, keys_ref, vals_ref, own_q_ref,
    seg_ref, dest_ref, row_ref, table_ref, clen_ref,
    fresh_ref, pool_ref, kv_ref, scr_ref, sems,
):
    heads, page, pages, rows, steps, pages_max, requests = sizes
    copies = [
        pltpu.make_async_copy(source, target, sems.at[i])
        for i, (source, target) in enumerate((
            (seg_hbm, seg_ref), (dest_hbm, dest_ref), (row_hbm, row_ref),
            (kv_hbm, kv_ref), (table_hbm, table_ref), (clen_hbm, clen_ref),
            (q_hbm, own_q_ref), (fresh_hbm, fresh_ref.at[: fresh_hbm.shape[0]]),
            (pool_hbm, pool_ref),
        ))
    ]
    if fresh_ref.shape[0] > fresh_hbm.shape[0]:
        fresh_ref[fresh_hbm.shape[0] :, :] = jnp.zeros(
            (fresh_ref.shape[0] - fresh_hbm.shape[0], LANES), fresh_ref.dtype
        )
    for copy in copies:
        copy.start()
    total_ref[...] = jnp.ones_like(total_ref)
    span = pages * page

    for r in range(requests):
        info_ref[0, r] = 0
        info_ref[1, r] = 0
        info_ref[2, r] = -1
        info_ref[3, r] = 0
    for copy in copies[:3]:
        copy.wait()
    length = len_ref[0]
    info_ref[5, 0] = length
    for p in reversed(range(pages)):
        r = seg_ref[0, p]
        info_ref[0, r] = p * page
        info_ref[2, r] = jnp.where(p * page < length, dest_ref[0, p], -1)
        info_ref[3, r] = row_ref[0, p]
    for p in range(pages):
        r = seg_ref[0, p]
        info_ref[1, r] = jnp.minimum((p + 1) * page, length)
        info_ref[4, p] = info_ref[0, r]

    copies[3].wait()
    for part, out_ref in enumerate((keys_ref, vals_ref)):
        if heads == 1:
            out_ref[...] = kv_ref[part * span : (part + 1) * span, :]
        else:
            scr_ref[...] = kv_ref[part * span * heads : (part + 1) * span * heads, :].astype(
                jnp.float32
            )
            for h in range(heads):
                out_ref[:, h * LANES : (h + 1) * LANES] = scr_ref[
                    pl.ds(h, span, stride=heads), :
                ].astype(jnp.bfloat16)

    for copy in copies[4:]:
        copy.wait()
    scale2 = LANES**-0.5 * LOG2E
    per_row = own_q_ref.shape[0] // rows
    groups = per_row // (steps * heads)
    fresh = fresh_ref[...]
    width = fresh.shape[0]
    page_rows = page * heads

    col = lax.broadcasted_iota(jnp.int32, (per_row, width), 1)
    sub = lax.broadcasted_iota(jnp.int32, (per_row, width), 0)
    fresh_ok = (
        ((col // heads) % 2 == 0)
        & ((col // (2 * heads)) % steps <= sub // (groups * heads))
        & (col % heads == sub % heads)
    )
    fresh_row = jnp.where(fresh_ok, col // (2 * heads * steps), -1)
    ccol = lax.broadcasted_iota(jnp.int32, (per_row, pages_max * page_rows), 1)
    csub = lax.broadcasted_iota(jnp.int32, (per_row, pages_max * page_rows), 0)
    far = rows * pages_max * page
    token = jnp.where(ccol % heads == csub % heads, ccol // heads, far)

    def gather(b, part):
        pieces = []
        for j in range(pages_max):
            spot = (table_ref[0, b * pages_max + j] * 2 + part) * page_rows
            pieces.append(pool_ref[pl.ds(pl.multiple_of(spot, page_rows), page_rows), :])
        return jnp.concatenate(pieces, axis=0)

    def row_slice(b):
        return slice(b * per_row, (b + 1) * per_row)

    fresh_scores = [dot_nt(own_q_ref[row_slice(b), :], fresh) for b in range(rows)]
    scores = [dot_nt(own_q_ref[row_slice(b), :], gather(b, 0)) for b in range(rows)]
    cache_terms, fresh_terms, totals = [], [], []
    for b in range(rows):
        s_c = jnp.where(token < clen_ref[0, b], scores[b], NEGATIVE)
        s_f = jnp.where(fresh_row == b, fresh_scores[b], NEGATIVE)
        pieces = [s_c[:, i : i + width] for i in range(0, s_c.shape[1], width)] + [s_f]
        top = functools.reduce(jnp.maximum, pieces)
        top = jnp.max(top, axis=1, keepdims=True)
        weights = [jnp.exp2((piece - top) * scale2) for piece in pieces]
        total = jnp.sum(functools.reduce(jnp.add, weights), axis=1, keepdims=True)
        cache_terms.append(two_terms(jnp.concatenate(weights[:-1], axis=1)))
        fresh_terms.append(pltpu.roll(weights[-1], heads, 1))
        totals.append(total)
        lse = top * scale2 + jnp.log2(total)
        lse_ref[row_slice(b), :] = jnp.broadcast_to(lse, (per_row, LANES))
    count = rows * per_row
    fresh_acc = dot_nn(two_terms(jnp.concatenate(fresh_terms, axis=0)), fresh)
    fresh_acc = fresh_acc[:count] + fresh_acc[count:]
    for b in range(rows):
        acc = dot_nn(cache_terms[b], gather(b, 1))
        acc = acc[:per_row] + acc[per_row:] + fresh_acc[row_slice(b)]
        part_ref[row_slice(b), :] = acc * (1.0 / totals[b])


def pages_kernel(sizes, partners, info_ref, *refs):
    heads, page, pages, rows, requests, capacity, instances = sizes
    slot_count = 1 if partners is None else len(partners)
    slots = refs[:slot_count]
    keys_ref, vals_ref, _, own_ref, send_ref, token_ref, q_scr = refs[slot_count:]
    me = lax.axis_index("inst")
    span = pages * page
    scale2 = LANES**-0.5 * LOG2E
    count = own_ref.shape[0]
    per_row = count // requests
    token_ref[...] = jnp.zeros_like(token_ref)
    for r in range(requests):
        dest, row = info_ref[2, r], info_ref[3, r]
        place = slice(r * per_row, (r + 1) * per_row)
        if partners is None:
            start = pl.multiple_of((jnp.maximum(dest, 0) * rows + row) * per_row, per_row)
            q_scr[place, :] = slots[0][pl.ds(start, per_row), :]
        else:
            start = pl.multiple_of(row * per_row, per_row)
            picked = slots[0][pl.ds(start, per_row), :]
            for k, offset in enumerate(partners[1:]):
                other = slots[k + 1][pl.ds(start, per_row), :]
                picked = jnp.where(dest == jnp.bitwise_xor(me, offset), other, picked)
            q_scr[place, :] = picked

    cut = capacity * page
    totals, tops, accs = [], [], []
    for low, high, first, last in ((0, cut, 0, 1), (cut, span, 1, requests)):
        wide = high - low
        scores = dot_nt(
            spread_heads(q_scr[first * per_row : last * per_row, :], heads), keys_ref[low:high, :]
        )
        token = low + lax.broadcasted_iota(jnp.int32, (per_row, wide), 1)
        weights = []
        for r in range(first, last):
            keep = (token >= info_ref[0, r]) & (token < info_ref[1, r])
            spot = (r - first) * per_row
            s_r = jnp.where(keep, scores[spot : spot + per_row], NEGATIVE)
            top = jnp.max(s_r, axis=1, keepdims=True)
            w_r = jnp.where(keep, jnp.exp2((s_r - top) * scale2), 0.0)
            weights.append(w_r)
            tops.append(top)
            totals.append(jnp.sum(w_r, axis=1, keepdims=True))
        acc = dot_nn(two_terms(jnp.concatenate(weights, axis=0)), vals_ref[low:high, :])
        half = (last - first) * per_row
        accs.append(pick_head(acc[:half] + acc[half:], heads))
    acc = jnp.concatenate(accs, axis=0)
    total = jnp.concatenate(totals, axis=0)
    live = total > 0.0
    blended = jnp.where(live, acc / jnp.where(live, total, 1.0), 0.0)
    lse = jnp.where(
        live,
        jnp.concatenate(tops, axis=0) * scale2 + jnp.log2(jnp.where(live, total, 1.0)),
        NEGATIVE,
    )
    own_ref[...] = blended
    send_ref[:count, :] = blended.astype(jnp.bfloat16)
    blocks = -(-count // LANES)
    lines = []
    for j in range(blocks):
        piece = lse[j * LANES : min((j + 1) * LANES, count)]
        shape = (piece.shape[0], LANES)
        same = lax.broadcasted_iota(jnp.int32, shape, 0) == lax.broadcasted_iota(
            jnp.int32, shape, 1
        )
        lines.append(jnp.sum(jnp.where(same, piece, 0.0), axis=0, keepdims=True))
    line = jnp.concatenate(lines, axis=0)
    first = line.astype(jnp.bfloat16)
    rest = line - first.astype(jnp.float32)
    second = rest.astype(jnp.bfloat16)
    third = (rest - second.astype(jnp.float32)).astype(jnp.bfloat16)
    terms = [t.astype(jnp.float32) for t in (first, second, third)]
    lane = lax.broadcasted_iota(jnp.int32, (1, LANES), 1)
    for f in (2, 3):
        tags = jnp.full((1, LANES), -1, jnp.int32)
        for r in range(requests):
            tags = jnp.where(lane == r, info_ref[f, r], tags)
        terms.append(tags.astype(jnp.float32))
    spare = send_ref.shape[0] - count
    terms.append(jnp.zeros((spare - 3 * blocks - 2, LANES), jnp.float32))
    send_ref[count:, :] = jnp.concatenate(terms, axis=0).astype(jnp.bfloat16)


def prefill_kernel(sizes, first_tile, info_ref, q_ref, keys_ref, vals_ref, *refs):
    heads, page, pages, block = sizes
    out_ref, token_ref, lag_ref = refs[-3:]
    tile = pl.program_id(0) + first_tile
    token_ref[...] = jnp.zeros_like(token_ref)
    page_rows = out_ref.shape[0] * page // block
    per_token = page_rows // page
    per_block = block // page
    scale2 = LANES**-0.5 * LOG2E
    length = info_ref[5, 0]

    @pl.when(tile == first_tile)
    def _():
        lane = lax.broadcasted_iota(jnp.int32, lag_ref.shape, 1)
        lag_ref[...] = lane - lax.broadcasted_iota(jnp.int32, lag_ref.shape, 0) // per_token

    first_key = info_ref[4, tile * per_block]
    first_block = first_key // block
    behind = tile - first_block

    def attend(count):
        base = (tile - (count - 1)) * block
        keys = keys_ref[pl.ds(pl.multiple_of(base, block), count * block), :]
        vals = vals_ref[pl.ds(pl.multiple_of(base, block), count * block), :]
        lane = lax.broadcasted_iota(jnp.int32, (1, block), 1)
        def score(p):
            rows = slice(p * page_rows, (p + 1) * page_rows)
            return dot_nt(spread_heads(q_ref[rows, :], heads), keys)

        ahead = score(0)
        for p in range(per_block):
            rows = slice(p * page_rows, (p + 1) * page_rows)
            scores = ahead
            if p + 1 < per_block:
                ahead = score(p + 1)
            start = info_ref[4, tile * per_block + p] - base
            pieces = []
            for j in range(count):
                s_j = scores[:, j * block : (j + 1) * block]
                keep = lane >= start - j * block
                if j == count - 1:
                    keep = keep & (lag_ref[...] <= p * page)
                pieces.append(jnp.where(keep, s_j, NEGATIVE))
            top = pieces[0]
            for piece in pieces[1:]:
                top = jnp.maximum(top, piece)
            top = jnp.max(top, axis=1, keepdims=True)
            weights = [jnp.exp2((piece - top) * scale2) for piece in pieces]
            total = weights[0]
            for w_j in weights[1:]:
                total = total + w_j
            total = jnp.sum(total, axis=1, keepdims=True)
            joined = jnp.concatenate([w_j.astype(jnp.bfloat16) for w_j in weights], axis=1)
            acc = pick_head(dot_nn(joined, vals), heads)
            place = lax.broadcasted_iota(jnp.int32, (page_rows, 1), 0) // per_token
            live = place < length - (tile * block + p * page)
            out_ref[rows, :] = (acc * jnp.where(live, 1.0 / total, 0.0)).astype(jnp.bfloat16)

    longest = 3
    for count in range(1, longest + 1):
        pl.when(behind == count - 1)(functools.partial(attend, count))


def join_kernel(sizes, with_own, last, *refs):
    rows, requests, blocks_of = sizes
    sent_count = len(blocks_of)
    refs = list(refs)
    own_ref = refs.pop(0) if with_own else None
    sent, refs = refs[:sent_count], refs[sent_count:]
    top_in, total_in, acc_in = refs[:3]
    refs = refs[4:]
    if last:
        out_ref, top_scr, total_scr, acc_scr, tag_scr, tags, sem = refs
    else:
        top_scr, total_scr, acc_scr, token_ref, tag_scr, tags, sem = refs
        token_ref[...] = jnp.zeros_like(token_ref)
    me = lax.axis_index("inst")
    per_row = acc_in.shape[0] // rows
    count = requests * per_row
    blocks = -(-count // LANES)
    instances = sum(blocks_of)
    places = [(k, i) for k in range(sent_count) for i in range(blocks_of[k])]
    lines = []
    for n, (k, i) in enumerate(places):
        tall = sent[k].shape[0] // blocks_of[k]
        stats = sent[k][i * tall + count : (i + 1) * tall, :].astype(jnp.float32)
        lines.append(
            stats[:blocks] + stats[blocks : 2 * blocks] + stats[2 * blocks : 3 * blocks]
        )
        tag_scr[n : n + 1, :] = stats[3 * blocks : 3 * blocks + 1].astype(jnp.int32)
        tag_scr[instances + n : instances + n + 1, :] = stats[
            3 * blocks + 1 : 3 * blocks + 2
        ].astype(jnp.int32)
    copy = pltpu.make_async_copy(tag_scr, tags, sem)
    copy.start()
    top_scr[...] = top_in[...]
    total_scr[...] = total_in[...]
    acc_scr[...] = acc_in[...]
    lane = lax.broadcasted_iota(jnp.int32, (per_row, LANES), 1)
    sub = lax.broadcasted_iota(jnp.int32, (per_row, LANES), 0)
    copy.wait()
    for n, (k, i) in enumerate(places):
        tall = sent[k].shape[0] // blocks_of[k]
        for r in range(requests):

            @pl.when(tags[n, r] == me)
            def _():
                start = pl.multiple_of(tags[instances + n, r] * per_row, per_row)
                place = pl.ds(start, per_row)
                j, offset = divmod(r * per_row, LANES)
                spread = jnp.where(lane == sub + offset, lines[n][j : j + 1, :], 0.0)
                level = jnp.sum(spread, axis=1, keepdims=True)
                spot = r * per_row
                if with_own and n == 0:
                    values = own_ref[spot : spot + per_row, :]
                else:
                    spot = spot + i * tall
                    values = sent[k][spot : spot + per_row, :].astype(jnp.float32)
                top = top_scr[place, :]
                joined = jnp.maximum(top, level)
                old = jnp.exp2(top - joined)
                new = jnp.exp2(level - joined)
                top_scr[place, :] = joined
                total_scr[place, :] = total_scr[place, :] * old + new
                acc_scr[place, :] = acc_scr[place, :] * old + values * new

    if last:
        out_ref[...] = (acc_scr[...] / total_scr[...]).astype(jnp.bfloat16)


def swap(block, offset, instances):
    return lax.ppermute(block, "inst", [(i, i ^ offset) for i in range(instances)])


def gather_all(block):
    whole = lax.all_gather(block, "inst", axis=0)
    return whole.reshape((-1,) + block.shape[1:])


def in_hbm(field):
    return pltpu.with_memory_space_constraint(field, pltpu.HBM)


def params(**extra):
    return pltpu.CompilerParams(vmem_limit_bytes=VMEM_LIMIT, **extra)


def shards(
    instances,
    prefill_q,
    prefill_kv,
    span_len,
    page_seg,
    page_dest,
    page_row,
    dec_q,
    dec_new,
    cache_kv,
    block_table,
    cache_len,
):
    _, span, heads, width = prefill_q.shape
    pages = page_seg.shape[1]
    _, rows, steps = dec_q.shape[:3]
    pool, page = cache_kv.shape[1], cache_kv.shape[3]
    pages_max = block_table.shape[1] // rows
    capacity = -(-2 * pages // instances)
    requests = pages - capacity + 1
    groups = width // LANES
    per_row = steps * groups * heads
    block = LANES
    sizes = (heads, page, pages, rows, steps, pages_max, requests)
    dest = page_dest.reshape(1, pages)
    slot_width = 32
    f32, bf16, i32 = jnp.float32, jnp.bfloat16, jnp.int32
    shape = jax.ShapeDtypeStruct

    direct = instances <= DIRECT and instances & (instances - 1) == 0
    queries = query_rows(dec_q[0])
    if direct:
        arrived = {x: swap(queries, x, instances) for x in range(1, instances)}

    fresh = dec_new.reshape(-1, LANES)
    source_kv = prefill_kv.reshape(-1, LANES)
    cache = cache_kv.reshape(-1, LANES)
    ints = (page_seg, dest, page_row, block_table, cache_len)
    info, *state, keys, vals, own_q = pl.pallas_call(
        functools.partial(cache_kernel, sizes),
        out_shape=(
            shape((8, slot_width), i32),
            *[shape((rows * per_row, LANES), f32)] * 3,
            shape((span, heads * LANES), bf16),
            shape((span, heads * LANES), bf16),
            shape(queries.shape, bf16),
        ),
        in_specs=[SMEM_SPEC] + [HBM_SPEC] * 9,
        out_specs=(SMEM_SPEC,) + (VMEM_SPEC,) * 6,
        scratch_shapes=[pltpu.SMEM(x.shape, i32) for x in ints]
        + [
            pltpu.VMEM((-(-fresh.shape[0] // LANES) * LANES, LANES), bf16),
            pltpu.VMEM(cache.shape, bf16),
            pltpu.VMEM(source_kv.shape, bf16),
            pltpu.VMEM((span * heads, LANES), f32),
            pltpu.SemaphoreType.DMA((9,)),
        ],
        compiler_params=params(),
        cost_estimate=BRIEF,
        name="cache",
    )(span_len, *map(in_hbm, (*ints, queries, fresh, cache, source_kv)))
    count = requests * per_row
    tall = count + -(-(3 * -(-count // LANES) + 2) // 16) * 16
    token = shape((8, LANES), f32)

    def attend_pages(partners, slots, after):
        return pl.pallas_call(
            functools.partial(
                pages_kernel,
                (heads, page, pages, rows, requests, capacity, instances),
                partners,
            ),
            out_shape=(shape((count, LANES), f32), shape((tall, LANES), bf16), token),
            in_specs=[SMEM_SPEC] + [VMEM_SPEC] * (len(slots) + 2) + [ANY_SPEC],
            out_specs=(VMEM_SPEC,) * 3,
            scratch_shapes=[pltpu.VMEM((count, LANES), bf16)],
            compiler_params=params(),
            cost_estimate=BRIEF,
            name="pages",
        )(info, *slots, keys, vals, after)

    q_rows = query_rows(prefill_q[0])
    tile_rows = block * groups * heads
    tiles = span // block
    whole = lambda i: (0, 0)

    def attend_source(first, last, after, earlier=None):
        rest = [after] if earlier is None else [after, earlier]
        return pl.pallas_call(
            functools.partial(prefill_kernel, (heads, page, pages, block), first),
            out_shape=(shape(q_rows.shape, bf16), token),
            grid=(last - first,),
            in_specs=[SMEM_SPEC]
            + [
                pl.BlockSpec((tile_rows, LANES), lambda i: (i + first, 0)),
                pl.BlockSpec(keys.shape, whole),
                pl.BlockSpec(vals.shape, whole),
            ]
            + [ANY_SPEC] * len(rest),
            out_specs=(
                pl.BlockSpec((tile_rows, LANES), lambda i: (i + first, 0)),
                pl.BlockSpec(token.shape, whole),
            ),
            scratch_shapes=[pltpu.VMEM((page * groups * heads, block), i32)],
            input_output_aliases={} if earlier is None else {5: 0},
            compiler_params=params(),
            cost_estimate=BRIEF,
            name="prefill",
        )(info, q_rows, keys, vals, *rest)

    def join(own, sent, state, after, last):
        blocks_of = tuple(block.shape[0] // tall for block in sent)
        tag_rows = -(-2 * sum(blocks_of) // 8) * 8
        lead = [] if own is None else [own]
        whole_state = [shape((rows * per_row, LANES), f32)] * 3
        result = shape((rows * per_row, LANES), bf16)
        return pl.pallas_call(
            functools.partial(join_kernel, (rows, requests, blocks_of), own is not None, last),
            out_shape=result if last else (*whole_state, token),
            in_specs=[VMEM_SPEC] * (len(lead) + len(sent) + 3) + [ANY_SPEC],
            out_specs=VMEM_SPEC if last else (VMEM_SPEC,) * 4,
            scratch_shapes=[pltpu.VMEM(x.shape, f32) for x in whole_state if last]
            + [
                pltpu.VMEM((tag_rows, LANES), i32),
                pltpu.SMEM((tag_rows, LANES), i32),
                pltpu.SemaphoreType.DMA,
            ],
            compiler_params=params(),
            cost_estimate=BRIEF,
            name="join",
        )(*lead, *sent, *state, after)

    if direct and instances > 2:
        x, *near = range(instances - 1, 0, -1)
        own, block_own, done = attend_pages((0, x), [own_q, arrived[x]], state[0])
        far = swap(block_own, x, instances)
        prefill_out, done = attend_source(0, EARLY, done)
        _, sent, done = attend_pages(tuple(near), [arrived[x] for x in near], done)
        *state, done = join(own, [block_own, far], state, done, False)
        prefill_out, done = attend_source(EARLY, tiles, done, prefill_out)
        dec_out = join(None, [swap(sent, x, instances) for x in near], state, done, True)
    else:
        queries = gather_all(queries)
        own, sent, done = attend_pages(None, [queries], state[0])
        prefill_out, done = attend_source(0, tiles, done)
        dec_out = join(None, [gather_all(sent)], state, done, True)

    return (
        from_rows(prefill_out, prefill_q.shape),
        from_rows(dec_out, dec_q.shape),
    )


def solution(mesh):
    return jax.shard_map(
        functools.partial(shards, mesh.shape["inst"]),
        mesh=mesh,
        in_specs=(
            P(("pool", "inst"), None, "tp", None),
            P(("pool", "inst"), None, None, "tp", None),
            P(("pool", "inst")),
            P(("pool", "inst"), None),
            P(("pool", "inst"), None, None),
            P(("pool", "inst"), None),
            P(("pool", "inst"), None, None, "tp", None),
            P(("pool", "inst"), None, None, None, "tp", None),
            P(("pool", "inst"), None, None, None, "tp", None),
            P(("pool", "inst"), None),
            P(("pool", "inst"), None),
        ),
        out_specs=(
            P(("pool", "inst"), None, "tp", None),
            P(("pool", "inst"), None, None, "tp", None),
        ),
        check_vma=False,
    )
```

```python
import functools
import math

import jax
import jax.numpy as jnp
from jax import lax
from jax.experimental import pallas as pl
from jax.experimental.pallas import tpu as pltpu
from jax.sharding import PartitionSpec as P

NEGATIVE = -1e30
LOG2E = math.log2(math.e)
LANES = 128
DIRECT = 8
EARLY = 3
VMEM_LIMIT = 48 * 1024 * 1024

SMEM_SPEC = pl.BlockSpec(memory_space=pltpu.SMEM)
BRIEF = pl.CostEstimate(flops=1000, bytes_accessed=1000, transcendentals=0)
ANY_SPEC = pl.BlockSpec(memory_space=pl.ANY)
HBM_SPEC = pl.BlockSpec(memory_space=pltpu.HBM)
VMEM_SPEC = pl.BlockSpec(memory_space=pltpu.VMEM)


def query_rows(field):
    lead = math.prod(field.shape[:-2])
    heads, width = field.shape[-2:]
    split = field.reshape(lead, heads, width // LANES, LANES)
    return split.transpose(0, 2, 1, 3).reshape(-1, LANES)


def from_rows(rows, shape):
    heads, width = shape[-2:]
    lead = math.prod(shape[:-2])
    split = rows.reshape(lead, width // LANES, heads, LANES)
    return split.transpose(0, 2, 1, 3).reshape(shape)


def head_of(shape, axis, heads):
    return lax.broadcasted_iota(jnp.int32, shape, axis) % heads


def dot_nt(first, second):
    return lax.dot_general(
        first, second, (((1,), (1,)), ((), ())), preferred_element_type=jnp.float32
    )


def dot_nn(first, second):
    return jnp.dot(first, second, preferred_element_type=jnp.float32)


def two_terms(weights):
    upper = weights.astype(jnp.bfloat16)
    lower = (weights - upper.astype(jnp.float32)).astype(jnp.bfloat16)
    return jnp.concatenate([upper, lower], axis=0)


def spread_heads(rows, heads):
    if heads == 1:
        return rows
    owner = head_of((16, LANES), 0, heads)
    tall = rows.reshape(-1, 16, LANES)
    parts = []
    for h in range(heads):
        mark = jnp.where(owner == h, 1.0, 0.0).astype(rows.dtype)
        parts.append((tall * mark[None]).reshape(rows.shape))
    return jnp.concatenate(parts, axis=1)


def pick_head(wide, heads):
    if heads == 1:
        return wide
    owner = head_of((wide.shape[0], LANES), 0, heads)
    picked = wide[:, :LANES]
    for h in range(1, heads):
        picked = jnp.where(owner == h, wide[:, h * LANES : (h + 1) * LANES], picked)
    return picked


def cache_kernel(
    sizes, len_ref, seg_hbm, dest_hbm, row_hbm, table_hbm, clen_hbm,
    q_hbm, fresh_hbm, pool_hbm, kv_hbm,
    info_ref, lse_ref, total_ref, part_ref, keys_ref, vals_ref, own_q_ref,
    seg_ref, dest_ref, row_ref, table_ref, clen_ref,
    fresh_ref, pool_ref, kv_ref, scr_ref, sems,
):
    heads, page, pages, rows, steps, pages_max, requests = sizes
    copies = [
        pltpu.make_async_copy(source, target, sems.at[i])
        for i, (source, target) in enumerate((
            (seg_hbm, seg_ref), (dest_hbm, dest_ref), (row_hbm, row_ref),
            (kv_hbm, kv_ref), (table_hbm, table_ref), (clen_hbm, clen_ref),
            (q_hbm, own_q_ref), (fresh_hbm, fresh_ref.at[: fresh_hbm.shape[0]]),
            (pool_hbm, pool_ref),
        ))
    ]
    if fresh_ref.shape[0] > fresh_hbm.shape[0]:
        fresh_ref[fresh_hbm.shape[0] :, :] = jnp.zeros(
            (fresh_ref.shape[0] - fresh_hbm.shape[0], LANES), fresh_ref.dtype
        )
    for copy in copies:
        copy.start()
    total_ref[...] = jnp.ones_like(total_ref)
    span = pages * page

    for r in range(requests):
        info_ref[0, r] = 0
        info_ref[1, r] = 0
        info_ref[2, r] = -1
        info_ref[3, r] = 0
    for copy in copies[:3]:
        copy.wait()
    length = len_ref[0]
    info_ref[5, 0] = length
    for p in reversed(range(pages)):
        r = seg_ref[0, p]
        info_ref[0, r] = p * page
        info_ref[2, r] = jnp.where(p * page < length, dest_ref[0, p], -1)
        info_ref[3, r] = row_ref[0, p]
    for p in range(pages):
        r = seg_ref[0, p]
        info_ref[1, r] = jnp.minimum((p + 1) * page, length)
        info_ref[4, p] = info_ref[0, r]

    copies[3].wait()
    for part, out_ref in enumerate((keys_ref, vals_ref)):
        if heads == 1:
            out_ref[...] = kv_ref[part * span : (part + 1) * span, :]
        else:
            scr_ref[...] = kv_ref[part * span * heads : (part + 1) * span * heads, :].astype(
                jnp.float32
            )
            for h in range(heads):
                out_ref[:, h * LANES : (h + 1) * LANES] = scr_ref[
                    pl.ds(h, span, stride=heads), :
                ].astype(jnp.bfloat16)

    for copy in copies[4:]:
        copy.wait()
    scale2 = LANES**-0.5 * LOG2E
    per_row = own_q_ref.shape[0] // rows
    groups = per_row // (steps * heads)
    fresh = fresh_ref[...]
    width = fresh.shape[0]
    page_rows = page * heads

    col = lax.broadcasted_iota(jnp.int32, (per_row, width), 1)
    sub = lax.broadcasted_iota(jnp.int32, (per_row, width), 0)
    fresh_ok = (
        ((col // heads) % 2 == 0)
        & ((col // (2 * heads)) % steps <= sub // (groups * heads))
        & (col % heads == sub % heads)
    )
    fresh_row = jnp.where(fresh_ok, col // (2 * heads * steps), -1)
    ccol = lax.broadcasted_iota(jnp.int32, (per_row, pages_max * page_rows), 1)
    csub = lax.broadcasted_iota(jnp.int32, (per_row, pages_max * page_rows), 0)
    far = rows * pages_max * page
    token = jnp.where(ccol % heads == csub % heads, ccol // heads, far)

    def gather(b, part):
        pieces = []
        for j in range(pages_max):
            spot = (table_ref[0, b * pages_max + j] * 2 + part) * page_rows
            pieces.append(pool_ref[pl.ds(pl.multiple_of(spot, page_rows), page_rows), :])
        return jnp.concatenate(pieces, axis=0)

    def row_slice(b):
        return slice(b * per_row, (b + 1) * per_row)

    fresh_scores = [dot_nt(own_q_ref[row_slice(b), :], fresh) for b in range(rows)]
    scores = [dot_nt(own_q_ref[row_slice(b), :], gather(b, 0)) for b in range(rows)]
    cache_terms, fresh_terms, totals = [], [], []
    for b in range(rows):
        s_c = jnp.where(token < clen_ref[0, b], scores[b], NEGATIVE)
        s_f = jnp.where(fresh_row == b, fresh_scores[b], NEGATIVE)
        pieces = [s_c[:, i : i + width] for i in range(0, s_c.shape[1], width)] + [s_f]
        top = functools.reduce(jnp.maximum, pieces)
        top = jnp.max(top, axis=1, keepdims=True)
        weights = [jnp.exp2((piece - top) * scale2) for piece in pieces]
        total = jnp.sum(functools.reduce(jnp.add, weights), axis=1, keepdims=True)
        cache_terms.append(two_terms(jnp.concatenate(weights[:-1], axis=1)))
        fresh_terms.append(pltpu.roll(weights[-1], heads, 1))
        totals.append(total)
        lse = top * scale2 + jnp.log2(total)
        lse_ref[row_slice(b), :] = jnp.broadcast_to(lse, (per_row, LANES))
    count = rows * per_row
    fresh_acc = dot_nn(two_terms(jnp.concatenate(fresh_terms, axis=0)), fresh)
    fresh_acc = fresh_acc[:count] + fresh_acc[count:]
    for b in range(rows):
        acc = dot_nn(cache_terms[b], gather(b, 1))
        acc = acc[:per_row] + acc[per_row:] + fresh_acc[row_slice(b)]
        part_ref[row_slice(b), :] = acc * (1.0 / totals[b])


def pages_kernel(sizes, partners, info_ref, *refs):
    heads, page, pages, rows, requests, capacity, instances = sizes
    slot_count = 1 if partners is None else len(partners)
    slots = refs[:slot_count]
    keys_ref, vals_ref, _, own_ref, send_ref, token_ref, q_scr = refs[slot_count:]
    me = lax.axis_index("inst")
    span = pages * page
    scale2 = LANES**-0.5 * LOG2E
    count = own_ref.shape[0]
    per_row = count // requests
    token_ref[...] = jnp.zeros_like(token_ref)
    for r in range(requests):
        dest, row = info_ref[2, r], info_ref[3, r]
        place = slice(r * per_row, (r + 1) * per_row)
        if partners is None:
            start = pl.multiple_of((jnp.maximum(dest, 0) * rows + row) * per_row, per_row)
            q_scr[place, :] = slots[0][pl.ds(start, per_row), :]
        else:
            start = pl.multiple_of(row * per_row, per_row)
            picked = slots[0][pl.ds(start, per_row), :]
            for k, offset in enumerate(partners[1:]):
                other = slots[k + 1][pl.ds(start, per_row), :]
                picked = jnp.where(dest == jnp.bitwise_xor(me, offset), other, picked)
            q_scr[place, :] = picked

    cut = capacity * page
    totals, tops, accs = [], [], []
    for low, high, first, last in ((0, cut, 0, 1), (cut, span, 1, requests)):
        wide = high - low
        scores = dot_nt(
            spread_heads(q_scr[first * per_row : last * per_row, :], heads), keys_ref[low:high, :]
        )
        token = low + lax.broadcasted_iota(jnp.int32, (per_row, wide), 1)
        weights = []
        for r in range(first, last):
            keep = (token >= info_ref[0, r]) & (token < info_ref[1, r])
            spot = (r - first) * per_row
            s_r = jnp.where(keep, scores[spot : spot + per_row], NEGATIVE)
            top = jnp.max(s_r, axis=1, keepdims=True)
            w_r = jnp.where(keep, jnp.exp2((s_r - top) * scale2), 0.0)
            weights.append(w_r)
            tops.append(top)
            totals.append(jnp.sum(w_r, axis=1, keepdims=True))
        acc = dot_nn(two_terms(jnp.concatenate(weights, axis=0)), vals_ref[low:high, :])
        half = (last - first) * per_row
        accs.append(pick_head(acc[:half] + acc[half:], heads))
    acc = jnp.concatenate(accs, axis=0)
    total = jnp.concatenate(totals, axis=0)
    live = total > 0.0
    blended = jnp.where(live, acc / jnp.where(live, total, 1.0), 0.0)
    lse = jnp.where(
        live,
        jnp.concatenate(tops, axis=0) * scale2 + jnp.log2(jnp.where(live, total, 1.0)),
        NEGATIVE,
    )
    own_ref[...] = blended
    send_ref[:count, :] = blended.astype(jnp.bfloat16)
    blocks = -(-count // LANES)
    lines = []
    for j in range(blocks):
        piece = lse[j * LANES : min((j + 1) * LANES, count)]
        shape = (piece.shape[0], LANES)
        same = lax.broadcasted_iota(jnp.int32, shape, 0) == lax.broadcasted_iota(
            jnp.int32, shape, 1
        )
        lines.append(jnp.sum(jnp.where(same, piece, 0.0), axis=0, keepdims=True))
    line = jnp.concatenate(lines, axis=0)
    first = line.astype(jnp.bfloat16)
    rest = line - first.astype(jnp.float32)
    second = rest.astype(jnp.bfloat16)
    third = (rest - second.astype(jnp.float32)).astype(jnp.bfloat16)
    terms = [t.astype(jnp.float32) for t in (first, second, third)]
    lane = lax.broadcasted_iota(jnp.int32, (1, LANES), 1)
    for f in (2, 3):
        tags = jnp.full((1, LANES), -1, jnp.int32)
        for r in range(requests):
            tags = jnp.where(lane == r, info_ref[f, r], tags)
        terms.append(tags.astype(jnp.float32))
    spare = send_ref.shape[0] - count
    terms.append(jnp.zeros((spare - 3 * blocks - 2, LANES), jnp.float32))
    send_ref[count:, :] = jnp.concatenate(terms, axis=0).astype(jnp.bfloat16)


def prefill_kernel(sizes, first_tile, info_ref, q_ref, keys_ref, vals_ref, *refs):
    heads, page, pages, block = sizes
    out_ref, token_ref, lag_ref = refs[-3:]
    tile = pl.program_id(0) + first_tile
    token_ref[...] = jnp.zeros_like(token_ref)
    page_rows = out_ref.shape[0] * page // block
    per_token = page_rows // page
    per_block = block // page
    scale2 = LANES**-0.5 * LOG2E
    length = info_ref[5, 0]

    @pl.when(tile == first_tile)
    def _():
        lane = lax.broadcasted_iota(jnp.int32, lag_ref.shape, 1)
        lag_ref[...] = lane - lax.broadcasted_iota(jnp.int32, lag_ref.shape, 0) // per_token

    first_key = info_ref[4, tile * per_block]
    first_block = first_key // block
    behind = tile - first_block

    def attend(count):
        base = (tile - (count - 1)) * block
        keys = keys_ref[pl.ds(pl.multiple_of(base, block), count * block), :]
        vals = vals_ref[pl.ds(pl.multiple_of(base, block), count * block), :]
        lane = lax.broadcasted_iota(jnp.int32, (1, block), 1)
        def score(p):
            rows = slice(p * page_rows, (p + 1) * page_rows)
            return dot_nt(spread_heads(q_ref[rows, :], heads), keys)

        ahead = score(0)
        for p in range(per_block):
            rows = slice(p * page_rows, (p + 1) * page_rows)
            scores = ahead
            if p + 1 < per_block:
                ahead = score(p + 1)
            start = info_ref[4, tile * per_block + p] - base
            pieces = []
            for j in range(count):
                s_j = scores[:, j * block : (j + 1) * block]
                keep = lane >= start - j * block
                if j == count - 1:
                    keep = keep & (lag_ref[...] <= p * page)
                pieces.append(jnp.where(keep, s_j, NEGATIVE))
            top = pieces[0]
            for piece in pieces[1:]:
                top = jnp.maximum(top, piece)
            top = jnp.max(top, axis=1, keepdims=True)
            weights = [jnp.exp2((piece - top) * scale2) for piece in pieces]
            total = weights[0]
            for w_j in weights[1:]:
                total = total + w_j
            total = jnp.sum(total, axis=1, keepdims=True)
            joined = jnp.concatenate([w_j.astype(jnp.bfloat16) for w_j in weights], axis=1)
            acc = pick_head(dot_nn(joined, vals), heads)
            place = lax.broadcasted_iota(jnp.int32, (page_rows, 1), 0) // per_token
            live = place < length - (tile * block + p * page)
            out_ref[rows, :] = (acc * jnp.where(live, 1.0 / total, 0.0)).astype(jnp.bfloat16)

    longest = 3
    for count in range(1, longest + 1):
        pl.when(behind == count - 1)(functools.partial(attend, count))


def join_kernel(sizes, with_own, last, *refs):
    rows, requests, blocks_of = sizes
    sent_count = len(blocks_of)
    refs = list(refs)
    own_ref = refs.pop(0) if with_own else None
    sent, refs = refs[:sent_count], refs[sent_count:]
    top_in, total_in, acc_in = refs[:3]
    refs = refs[4:]
    if last:
        out_ref, top_scr, total_scr, acc_scr, tag_scr, tags, sem = refs
    else:
        top_scr, total_scr, acc_scr, token_ref, tag_scr, tags, sem = refs
        token_ref[...] = jnp.zeros_like(token_ref)
    me = lax.axis_index("inst")
    per_row = acc_in.shape[0] // rows
    count = requests * per_row
    blocks = -(-count // LANES)
    instances = sum(blocks_of)
    places = [(k, i) for k in range(sent_count) for i in range(blocks_of[k])]
    lines = []
    for n, (k, i) in enumerate(places):
        tall = sent[k].shape[0] // blocks_of[k]
        stats = sent[k][i * tall + count : (i + 1) * tall, :].astype(jnp.float32)
        lines.append(
            stats[:blocks] + stats[blocks : 2 * blocks] + stats[2 * blocks : 3 * blocks]
        )
        tag_scr[n : n + 1, :] = stats[3 * blocks : 3 * blocks + 1].astype(jnp.int32)
        tag_scr[instances + n : instances + n + 1, :] = stats[
            3 * blocks + 1 : 3 * blocks + 2
        ].astype(jnp.int32)
    copy = pltpu.make_async_copy(tag_scr, tags, sem)
    copy.start()
    top_scr[...] = top_in[...]
    total_scr[...] = total_in[...]
    acc_scr[...] = acc_in[...]
    lane = lax.broadcasted_iota(jnp.int32, (per_row, LANES), 1)
    sub = lax.broadcasted_iota(jnp.int32, (per_row, LANES), 0)
    copy.wait()
    for n, (k, i) in enumerate(places):
        tall = sent[k].shape[0] // blocks_of[k]
        for r in range(requests):

            @pl.when(tags[n, r] == me)
            def _():
                start = pl.multiple_of(tags[instances + n, r] * per_row, per_row)
                place = pl.ds(start, per_row)
                j, offset = divmod(r * per_row, LANES)
                spread = jnp.where(lane == sub + offset, lines[n][j : j + 1, :], 0.0)
                level = jnp.sum(spread, axis=1, keepdims=True)
                spot = r * per_row
                if with_own and n == 0:
                    values = own_ref[spot : spot + per_row, :]
                else:
                    spot = spot + i * tall
                    values = sent[k][spot : spot + per_row, :].astype(jnp.float32)
                top = top_scr[place, :]
                joined = jnp.maximum(top, level)
                old = jnp.exp2(top - joined)
                new = jnp.exp2(level - joined)
                top_scr[place, :] = joined
                total_scr[place, :] = total_scr[place, :] * old + new
                acc_scr[place, :] = acc_scr[place, :] * old + values * new

    if last:
        out_ref[...] = (acc_scr[...] / total_scr[...]).astype(jnp.bfloat16)


def swap(block, offset, instances):
    return lax.ppermute(block, "inst", [(i, i ^ offset) for i in range(instances)])


def gather_all(block):
    whole = lax.all_gather(block, "inst", axis=0)
    return whole.reshape((-1,) + block.shape[1:])


def in_hbm(field):
    return pltpu.with_memory_space_constraint(field, pltpu.HBM)


def params(**extra):
    return pltpu.CompilerParams(vmem_limit_bytes=VMEM_LIMIT, **extra)


def shards(
    instances,
    prefill_q,
    prefill_kv,
    span_len,
    page_seg,
    page_dest,
    page_row,
    dec_q,
    dec_new,
    cache_kv,
    block_table,
    cache_len,
):
    _, span, heads, width = prefill_q.shape
    pages = page_seg.shape[1]
    _, rows, steps = dec_q.shape[:3]
    pool, page = cache_kv.shape[1], cache_kv.shape[3]
    pages_max = block_table.shape[1] // rows
    capacity = -(-2 * pages // instances)
    requests = pages - capacity + 1
    groups = width // LANES
    per_row = steps * groups * heads
    block = LANES
    sizes = (heads, page, pages, rows, steps, pages_max, requests)
    dest = page_dest.reshape(1, pages)
    slot_width = 32
    f32, bf16, i32 = jnp.float32, jnp.bfloat16, jnp.int32
    shape = jax.ShapeDtypeStruct

    direct = instances <= DIRECT and instances & (instances - 1) == 0
    queries = query_rows(dec_q[0])
    if direct:
        arrived = {x: swap(queries, x, instances) for x in range(1, instances)}

    fresh = dec_new.reshape(-1, LANES)
    source_kv = prefill_kv.reshape(-1, LANES)
    cache = cache_kv.reshape(-1, LANES)
    ints = (page_seg, dest, page_row, block_table, cache_len)
    info, *state, keys, vals, own_q = pl.pallas_call(
        functools.partial(cache_kernel, sizes),
        out_shape=(
            shape((8, slot_width), i32),
            *[shape((rows * per_row, LANES), f32)] * 3,
            shape((span, heads * LANES), bf16),
            shape((span, heads * LANES), bf16),
            shape(queries.shape, bf16),
        ),
        in_specs=[SMEM_SPEC] + [HBM_SPEC] * 9,
        out_specs=(SMEM_SPEC,) + (VMEM_SPEC,) * 6,
        scratch_shapes=[pltpu.SMEM(x.shape, i32) for x in ints]
        + [
            pltpu.VMEM((-(-fresh.shape[0] // LANES) * LANES, LANES), bf16),
            pltpu.VMEM(cache.shape, bf16),
            pltpu.VMEM(source_kv.shape, bf16),
            pltpu.VMEM((span * heads, LANES), f32),
            pltpu.SemaphoreType.DMA((9,)),
        ],
        compiler_params=params(),
        cost_estimate=BRIEF,
        name="cache",
    )(span_len, *map(in_hbm, (*ints, queries, fresh, cache, source_kv)))
    count = requests * per_row
    tall = count + -(-(3 * -(-count // LANES) + 2) // 16) * 16
    token = shape((8, LANES), f32)

    def attend_pages(partners, slots, after):
        return pl.pallas_call(
            functools.partial(
                pages_kernel,
                (heads, page, pages, rows, requests, capacity, instances),
                partners,
            ),
            out_shape=(shape((count, LANES), f32), shape((tall, LANES), bf16), token),
            in_specs=[SMEM_SPEC] + [VMEM_SPEC] * (len(slots) + 2) + [ANY_SPEC],
            out_specs=(VMEM_SPEC,) * 3,
            scratch_shapes=[pltpu.VMEM((count, LANES), bf16)],
            compiler_params=params(),
            cost_estimate=BRIEF,
            name="pages",
        )(info, *slots, keys, vals, after)

    q_rows = query_rows(prefill_q[0])
    tile_rows = block * groups * heads
    tiles = span // block
    whole = lambda i: (0, 0)

    def attend_source(first, last, after, earlier=None):
        rest = [after] if earlier is None else [after, earlier]
        return pl.pallas_call(
            functools.partial(prefill_kernel, (heads, page, pages, block), first),
            out_shape=(shape(q_rows.shape, bf16), token),
            grid=(last - first,),
            in_specs=[SMEM_SPEC]
            + [
                pl.BlockSpec((tile_rows, LANES), lambda i: (i + first, 0)),
                pl.BlockSpec(keys.shape, whole),
                pl.BlockSpec(vals.shape, whole),
            ]
            + [ANY_SPEC] * len(rest),
            out_specs=(
                pl.BlockSpec((tile_rows, LANES), lambda i: (i + first, 0)),
                pl.BlockSpec(token.shape, whole),
            ),
            scratch_shapes=[pltpu.VMEM((page * groups * heads, block), i32)],
            input_output_aliases={} if earlier is None else {5: 0},
            compiler_params=params(),
            cost_estimate=BRIEF,
            name="prefill",
        )(info, q_rows, keys, vals, *rest)

    def join(own, sent, state, after, last):
        blocks_of = tuple(block.shape[0] // tall for block in sent)
        tag_rows = -(-2 * sum(blocks_of) // 8) * 8
        lead = [] if own is None else [own]
        whole_state = [shape((rows * per_row, LANES), f32)] * 3
        result = shape((rows * per_row, LANES), bf16)
        return pl.pallas_call(
            functools.partial(join_kernel, (rows, requests, blocks_of), own is not None, last),
            out_shape=result if last else (*whole_state, token),
            in_specs=[VMEM_SPEC] * (len(lead) + len(sent) + 3) + [ANY_SPEC],
            out_specs=VMEM_SPEC if last else (VMEM_SPEC,) * 4,
            scratch_shapes=[pltpu.VMEM(x.shape, f32) for x in whole_state if last]
            + [
                pltpu.VMEM((tag_rows, LANES), i32),
                pltpu.SMEM((tag_rows, LANES), i32),
                pltpu.SemaphoreType.DMA,
            ],
            compiler_params=params(),
            cost_estimate=BRIEF,
            name="join",
        )(*lead, *sent, *state, after)

    if direct and instances > 2:
        x, *near = range(instances - 1, 0, -1)
        own, block_own, done = attend_pages((0, x), [own_q, arrived[x]], state[0])
        far = swap(block_own, x, instances)
        prefill_out, done = attend_source(0, EARLY, done)
        _, sent, done = attend_pages(tuple(near), [arrived[x] for x in near], done)
        *state, done = join(own, [block_own, far], state, done, False)
        prefill_out, done = attend_source(EARLY, tiles, done, prefill_out)
        dec_out = join(None, [swap(sent, x, instances) for x in near[::-1]], state, done, True)
    else:
        queries = gather_all(queries)
        own, sent, done = attend_pages(None, [queries], state[0])
        prefill_out, done = attend_source(0, tiles, done)
        dec_out = join(None, [gather_all(sent)], state, done, True)

    return (
        from_rows(prefill_out, prefill_q.shape),
        from_rows(dec_out, dec_q.shape),
    )


def solution(mesh):
    return jax.shard_map(
        functools.partial(shards, mesh.shape["inst"]),
        mesh=mesh,
        in_specs=(
            P(("pool", "inst"), None, "tp", None),
            P(("pool", "inst"), None, None, "tp", None),
            P(("pool", "inst")),
            P(("pool", "inst"), None),
            P(("pool", "inst"), None, None),
            P(("pool", "inst"), None),
            P(("pool", "inst"), None, None, "tp", None),
            P(("pool", "inst"), None, None, None, "tp", None),
            P(("pool", "inst"), None, None, None, "tp", None),
            P(("pool", "inst"), None),
            P(("pool", "inst"), None),
        ),
        out_specs=(
            P(("pool", "inst"), None, "tp", None),
            P(("pool", "inst"), None, None, "tp", None),
        ),
        check_vma=False,
    )
```

```python
import functools
import math

import jax
import jax.numpy as jnp
from jax import lax
from jax.experimental import pallas as pl
from jax.experimental.pallas import tpu as pltpu
from jax.sharding import PartitionSpec as P

NEGATIVE = -1e30
LOG2E = math.log2(math.e)
LANES = 128
DIRECT = 8
EARLY = 3
VMEM_LIMIT = 48 * 1024 * 1024

SMEM_SPEC = pl.BlockSpec(memory_space=pltpu.SMEM)
BRIEF = pl.CostEstimate(flops=1000, bytes_accessed=1000, transcendentals=0)
ANY_SPEC = pl.BlockSpec(memory_space=pl.ANY)
HBM_SPEC = pl.BlockSpec(memory_space=pltpu.HBM)
VMEM_SPEC = pl.BlockSpec(memory_space=pltpu.VMEM)


def query_rows(field):
    lead = math.prod(field.shape[:-2])
    heads, width = field.shape[-2:]
    split = field.reshape(lead, heads, width // LANES, LANES)
    return split.transpose(0, 2, 1, 3).reshape(-1, LANES)


def from_rows(rows, shape):
    heads, width = shape[-2:]
    lead = math.prod(shape[:-2])
    split = rows.reshape(lead, width // LANES, heads, LANES)
    return split.transpose(0, 2, 1, 3).reshape(shape)


def head_of(shape, axis, heads):
    return lax.broadcasted_iota(jnp.int32, shape, axis) % heads


def dot_nt(first, second):
    return lax.dot_general(
        first, second, (((1,), (1,)), ((), ())), preferred_element_type=jnp.float32
    )


def dot_nn(first, second):
    return jnp.dot(first, second, preferred_element_type=jnp.float32)


def two_terms(weights):
    upper = weights.astype(jnp.bfloat16)
    lower = (weights - upper.astype(jnp.float32)).astype(jnp.bfloat16)
    return jnp.concatenate([upper, lower], axis=0)


def spread_heads(rows, heads):
    if heads == 1:
        return rows
    owner = head_of((16, LANES), 0, heads)
    tall = rows.reshape(-1, 16, LANES)
    parts = []
    for h in range(heads):
        mark = jnp.where(owner == h, 1.0, 0.0).astype(rows.dtype)
        parts.append((tall * mark[None]).reshape(rows.shape))
    return jnp.concatenate(parts, axis=1)


def pick_head(wide, heads):
    if heads == 1:
        return wide
    owner = head_of((wide.shape[0], LANES), 0, heads)
    picked = wide[:, :LANES]
    for h in range(1, heads):
        picked = jnp.where(owner == h, wide[:, h * LANES : (h + 1) * LANES], picked)
    return picked


def cache_kernel(
    sizes, seg_hbm, dest_hbm, row_hbm, len_hbm, table_hbm, clen_hbm,
    q_hbm, fresh_hbm, pool_hbm, kv_hbm,
    info_ref, lse_ref, total_ref, part_ref, keys_ref, vals_ref, own_q_ref,
    seg_ref, dest_ref, row_ref, len_ref, table_ref, clen_ref,
    fresh_ref, pool_ref, kv_ref, scr_ref, sems,
):
    heads, page, pages, rows, steps, pages_max, requests = sizes
    copies = [
        pltpu.make_async_copy(source, target, sems.at[i])
        for i, (source, target) in enumerate((
            (seg_hbm, seg_ref), (dest_hbm, dest_ref), (row_hbm, row_ref), (len_hbm, len_ref),
            (kv_hbm, kv_ref), (table_hbm, table_ref), (clen_hbm, clen_ref),
            (q_hbm, own_q_ref), (fresh_hbm, fresh_ref.at[: fresh_hbm.shape[0]]),
            (pool_hbm, pool_ref),
        ))
    ]
    if fresh_ref.shape[0] > fresh_hbm.shape[0]:
        fresh_ref[fresh_hbm.shape[0] :, :] = jnp.zeros(
            (fresh_ref.shape[0] - fresh_hbm.shape[0], LANES), fresh_ref.dtype
        )
    for copy in copies:
        copy.start()
    total_ref[...] = jnp.ones_like(total_ref)
    span = pages * page

    for r in range(requests):
        info_ref[0, r] = 0
        info_ref[1, r] = 0
        info_ref[2, r] = -1
        info_ref[3, r] = 0
    for copy in copies[:4]:
        copy.wait()
    length = len_ref[0, 0]
    info_ref[5, 0] = length
    for p in reversed(range(pages)):
        r = seg_ref[0, p]
        info_ref[0, r] = p * page
        info_ref[2, r] = jnp.where(p * page < length, dest_ref[0, p], -1)
        info_ref[3, r] = row_ref[0, p]
    for p in range(pages):
        r = seg_ref[0, p]
        info_ref[1, r] = jnp.minimum((p + 1) * page, length)
        info_ref[4, p] = info_ref[0, r]

    copies[4].wait()
    for part, out_ref in enumerate((keys_ref, vals_ref)):
        if heads == 1:
            out_ref[...] = kv_ref[part * span : (part + 1) * span, :]
        else:
            scr_ref[...] = kv_ref[part * span * heads : (part + 1) * span * heads, :].astype(
                jnp.float32
            )
            for h in range(heads):
                out_ref[:, h * LANES : (h + 1) * LANES] = scr_ref[
                    pl.ds(h, span, stride=heads), :
                ].astype(jnp.bfloat16)

    for copy in copies[5:]:
        copy.wait()
    scale2 = LANES**-0.5 * LOG2E
    per_row = own_q_ref.shape[0] // rows
    groups = per_row // (steps * heads)
    fresh = fresh_ref[...]
    width = fresh.shape[0]
    page_rows = page * heads

    col = lax.broadcasted_iota(jnp.int32, (per_row, width), 1)
    sub = lax.broadcasted_iota(jnp.int32, (per_row, width), 0)
    fresh_ok = (
        ((col // heads) % 2 == 0)
        & ((col // (2 * heads)) % steps <= sub // (groups * heads))
        & (col % heads == sub % heads)
    )
    fresh_row = jnp.where(fresh_ok, col // (2 * heads * steps), -1)
    ccol = lax.broadcasted_iota(jnp.int32, (per_row, pages_max * page_rows), 1)
    csub = lax.broadcasted_iota(jnp.int32, (per_row, pages_max * page_rows), 0)
    far = rows * pages_max * page
    token = jnp.where(ccol % heads == csub % heads, ccol // heads, far)

    def gather(b, part):
        pieces = []
        for j in range(pages_max):
            spot = (table_ref[0, b * pages_max + j] * 2 + part) * page_rows
            pieces.append(pool_ref[pl.ds(pl.multiple_of(spot, page_rows), page_rows), :])
        return jnp.concatenate(pieces, axis=0)

    def row_slice(b):
        return slice(b * per_row, (b + 1) * per_row)

    fresh_scores = [dot_nt(own_q_ref[row_slice(b), :], fresh) for b in range(rows)]
    scores = [dot_nt(own_q_ref[row_slice(b), :], gather(b, 0)) for b in range(rows)]
    cache_terms, fresh_terms, totals = [], [], []
    for b in range(rows):
        s_c = jnp.where(token < clen_ref[0, b], scores[b], NEGATIVE)
        s_f = jnp.where(fresh_row == b, fresh_scores[b], NEGATIVE)
        pieces = [s_c[:, i : i + width] for i in range(0, s_c.shape[1], width)] + [s_f]
        top = functools.reduce(jnp.maximum, pieces)
        top = jnp.max(top, axis=1, keepdims=True)
        weights = [jnp.exp2((piece - top) * scale2) for piece in pieces]
        total = jnp.sum(functools.reduce(jnp.add, weights), axis=1, keepdims=True)
        cache_terms.append(two_terms(jnp.concatenate(weights[:-1], axis=1)))
        fresh_terms.append(pltpu.roll(weights[-1], heads, 1))
        totals.append(total)
        lse = top * scale2 + jnp.log2(total)
        lse_ref[row_slice(b), :] = jnp.broadcast_to(lse, (per_row, LANES))
    count = rows * per_row
    fresh_acc = dot_nn(two_terms(jnp.concatenate(fresh_terms, axis=0)), fresh)
    fresh_acc = fresh_acc[:count] + fresh_acc[count:]
    for b in range(rows):
        acc = dot_nn(cache_terms[b], gather(b, 1))
        acc = acc[:per_row] + acc[per_row:] + fresh_acc[row_slice(b)]
        part_ref[row_slice(b), :] = acc * (1.0 / totals[b])


def pages_kernel(sizes, partners, info_ref, *refs):
    heads, page, pages, rows, requests, capacity, instances = sizes
    slot_count = 1 if partners is None else len(partners)
    slots = refs[:slot_count]
    keys_ref, vals_ref, _, own_ref, send_ref, token_ref, q_scr = refs[slot_count:]
    me = lax.axis_index("inst")
    span = pages * page
    scale2 = LANES**-0.5 * LOG2E
    count = own_ref.shape[0]
    per_row = count // requests
    token_ref[...] = jnp.zeros_like(token_ref)
    for r in range(requests):
        dest, row = info_ref[2, r], info_ref[3, r]
        place = slice(r * per_row, (r + 1) * per_row)
        if partners is None:
            start = pl.multiple_of((jnp.maximum(dest, 0) * rows + row) * per_row, per_row)
            q_scr[place, :] = slots[0][pl.ds(start, per_row), :]
        else:
            start = pl.multiple_of(row * per_row, per_row)
            picked = slots[0][pl.ds(start, per_row), :]
            for k, offset in enumerate(partners[1:]):
                other = slots[k + 1][pl.ds(start, per_row), :]
                picked = jnp.where(dest == jnp.bitwise_xor(me, offset), other, picked)
            q_scr[place, :] = picked

    cut = capacity * page
    totals, tops, accs = [], [], []
    for low, high, first, last in ((0, cut, 0, 1), (cut, span, 1, requests)):
        wide = high - low
        scores = dot_nt(
            spread_heads(q_scr[first * per_row : last * per_row, :], heads), keys_ref[low:high, :]
        )
        token = low + lax.broadcasted_iota(jnp.int32, (per_row, wide), 1)
        weights = []
        for r in range(first, last):
            keep = (token >= info_ref[0, r]) & (token < info_ref[1, r])
            spot = (r - first) * per_row
            s_r = jnp.where(keep, scores[spot : spot + per_row], NEGATIVE)
            top = jnp.max(s_r, axis=1, keepdims=True)
            w_r = jnp.where(keep, jnp.exp2((s_r - top) * scale2), 0.0)
            weights.append(w_r)
            tops.append(top)
            totals.append(jnp.sum(w_r, axis=1, keepdims=True))
        acc = dot_nn(two_terms(jnp.concatenate(weights, axis=0)), vals_ref[low:high, :])
        half = (last - first) * per_row
        accs.append(pick_head(acc[:half] + acc[half:], heads))
    acc = jnp.concatenate(accs, axis=0)
    total = jnp.concatenate(totals, axis=0)
    live = total > 0.0
    blended = jnp.where(live, acc / jnp.where(live, total, 1.0), 0.0)
    lse = jnp.where(
        live,
        jnp.concatenate(tops, axis=0) * scale2 + jnp.log2(jnp.where(live, total, 1.0)),
        NEGATIVE,
    )
    own_ref[...] = blended
    send_ref[:count, :] = blended.astype(jnp.bfloat16)
    blocks = -(-count // LANES)
    lines = []
    for j in range(blocks):
        piece = lse[j * LANES : min((j + 1) * LANES, count)]
        shape = (piece.shape[0], LANES)
        same = lax.broadcasted_iota(jnp.int32, shape, 0) == lax.broadcasted_iota(
            jnp.int32, shape, 1
        )
        lines.append(jnp.sum(jnp.where(same, piece, 0.0), axis=0, keepdims=True))
    line = jnp.concatenate(lines, axis=0)
    first = line.astype(jnp.bfloat16)
    rest = line - first.astype(jnp.float32)
    second = rest.astype(jnp.bfloat16)
    third = (rest - second.astype(jnp.float32)).astype(jnp.bfloat16)
    terms = [t.astype(jnp.float32) for t in (first, second, third)]
    lane = lax.broadcasted_iota(jnp.int32, (1, LANES), 1)
    for f in (2, 3):
        tags = jnp.full((1, LANES), -1, jnp.int32)
        for r in range(requests):
            tags = jnp.where(lane == r, info_ref[f, r], tags)
        terms.append(tags.astype(jnp.float32))
    spare = send_ref.shape[0] - count
    terms.append(jnp.zeros((spare - 3 * blocks - 2, LANES), jnp.float32))
    send_ref[count:, :] = jnp.concatenate(terms, axis=0).astype(jnp.bfloat16)


def prefill_kernel(sizes, first_tile, info_ref, q_ref, keys_ref, vals_ref, *refs):
    heads, page, pages, block = sizes
    out_ref, token_ref, lag_ref = refs[-3:]
    tile = pl.program_id(0) + first_tile
    token_ref[...] = jnp.zeros_like(token_ref)
    page_rows = out_ref.shape[0] * page // block
    per_token = page_rows // page
    per_block = block // page
    scale2 = LANES**-0.5 * LOG2E
    length = info_ref[5, 0]

    @pl.when(tile == first_tile)
    def _():
        lane = lax.broadcasted_iota(jnp.int32, lag_ref.shape, 1)
        lag_ref[...] = lane - lax.broadcasted_iota(jnp.int32, lag_ref.shape, 0) // per_token

    first_key = info_ref[4, tile * per_block]
    first_block = first_key // block
    behind = tile - first_block

    def attend(count):
        base = (tile - (count - 1)) * block
        keys = keys_ref[pl.ds(pl.multiple_of(base, block), count * block), :]
        vals = vals_ref[pl.ds(pl.multiple_of(base, block), count * block), :]
        lane = lax.broadcasted_iota(jnp.int32, (1, block), 1)
        def score(p):
            rows = slice(p * page_rows, (p + 1) * page_rows)
            return dot_nt(spread_heads(q_ref[rows, :], heads), keys)

        ahead = score(0)
        for p in range(per_block):
            rows = slice(p * page_rows, (p + 1) * page_rows)
            scores = ahead
            if p + 1 < per_block:
                ahead = score(p + 1)
            start = info_ref[4, tile * per_block + p] - base
            pieces = []
            for j in range(count):
                s_j = scores[:, j * block : (j + 1) * block]
                keep = lane >= start - j * block
                if j == count - 1:
                    keep = keep & (lag_ref[...] <= p * page)
                pieces.append(jnp.where(keep, s_j, NEGATIVE))
            top = pieces[0]
            for piece in pieces[1:]:
                top = jnp.maximum(top, piece)
            top = jnp.max(top, axis=1, keepdims=True)
            weights = [jnp.exp2((piece - top) * scale2) for piece in pieces]
            total = weights[0]
            for w_j in weights[1:]:
                total = total + w_j
            total = jnp.sum(total, axis=1, keepdims=True)
            joined = jnp.concatenate([w_j.astype(jnp.bfloat16) for w_j in weights], axis=1)
            acc = pick_head(dot_nn(joined, vals), heads)
            place = lax.broadcasted_iota(jnp.int32, (page_rows, 1), 0) // per_token
            live = place < length - (tile * block + p * page)
            out_ref[rows, :] = (acc * jnp.where(live, 1.0 / total, 0.0)).astype(jnp.bfloat16)

    longest = 3
    for count in range(1, longest + 1):
        pl.when(behind == count - 1)(functools.partial(attend, count))


def join_kernel(sizes, with_own, last, *refs):
    rows, requests, blocks_of = sizes
    sent_count = len(blocks_of)
    refs = list(refs)
    own_ref = refs.pop(0) if with_own else None
    sent, refs = refs[:sent_count], refs[sent_count:]
    top_in, total_in, acc_in = refs[:3]
    refs = refs[4:]
    if last:
        out_ref, top_scr, total_scr, acc_scr, tag_scr, tags, sem = refs
    else:
        top_scr, total_scr, acc_scr, token_ref, tag_scr, tags, sem = refs
        token_ref[...] = jnp.zeros_like(token_ref)
    me = lax.axis_index("inst")
    per_row = acc_in.shape[0] // rows
    count = requests * per_row
    blocks = -(-count // LANES)
    instances = sum(blocks_of)
    places = [(k, i) for k in range(sent_count) for i in range(blocks_of[k])]
    lines = []
    for n, (k, i) in enumerate(places):
        tall = sent[k].shape[0] // blocks_of[k]
        stats = sent[k][i * tall + count : (i + 1) * tall, :].astype(jnp.float32)
        lines.append(
            stats[:blocks] + stats[blocks : 2 * blocks] + stats[2 * blocks : 3 * blocks]
        )
        tag_scr[n : n + 1, :] = stats[3 * blocks : 3 * blocks + 1].astype(jnp.int32)
        tag_scr[instances + n : instances + n + 1, :] = stats[
            3 * blocks + 1 : 3 * blocks + 2
        ].astype(jnp.int32)
    copy = pltpu.make_async_copy(tag_scr, tags, sem)
    copy.start()
    top_scr[...] = top_in[...]
    total_scr[...] = total_in[...]
    acc_scr[...] = acc_in[...]
    lane = lax.broadcasted_iota(jnp.int32, (per_row, LANES), 1)
    sub = lax.broadcasted_iota(jnp.int32, (per_row, LANES), 0)
    copy.wait()
    for n, (k, i) in enumerate(places):
        tall = sent[k].shape[0] // blocks_of[k]
        for r in range(requests):

            @pl.when(tags[n, r] == me)
            def _():
                start = pl.multiple_of(tags[instances + n, r] * per_row, per_row)
                place = pl.ds(start, per_row)
                j, offset = divmod(r * per_row, LANES)
                spread = jnp.where(lane == sub + offset, lines[n][j : j + 1, :], 0.0)
                level = jnp.sum(spread, axis=1, keepdims=True)
                spot = r * per_row
                if with_own and n == 0:
                    values = own_ref[spot : spot + per_row, :]
                else:
                    spot = spot + i * tall
                    values = sent[k][spot : spot + per_row, :].astype(jnp.float32)
                top = top_scr[place, :]
                joined = jnp.maximum(top, level)
                old = jnp.exp2(top - joined)
                new = jnp.exp2(level - joined)
                top_scr[place, :] = joined
                total_scr[place, :] = total_scr[place, :] * old + new
                acc_scr[place, :] = acc_scr[place, :] * old + values * new

    if last:
        out_ref[...] = (acc_scr[...] / total_scr[...]).astype(jnp.bfloat16)


def swap(block, offset, instances):
    return lax.ppermute(block, "inst", [(i, i ^ offset) for i in range(instances)])


def gather_all(block):
    whole = lax.all_gather(block, "inst", axis=0)
    return whole.reshape((-1,) + block.shape[1:])


def in_hbm(field):
    return pltpu.with_memory_space_constraint(field, pltpu.HBM)


def params(**extra):
    return pltpu.CompilerParams(vmem_limit_bytes=VMEM_LIMIT, **extra)


def shards(
    instances,
    prefill_q,
    prefill_kv,
    span_len,
    page_seg,
    page_dest,
    page_row,
    dec_q,
    dec_new,
    cache_kv,
    block_table,
    cache_len,
):
    _, span, heads, width = prefill_q.shape
    pages = page_seg.shape[1]
    _, rows, steps = dec_q.shape[:3]
    pool, page = cache_kv.shape[1], cache_kv.shape[3]
    pages_max = block_table.shape[1] // rows
    capacity = -(-2 * pages // instances)
    requests = pages - capacity + 1
    groups = width // LANES
    per_row = steps * groups * heads
    block = LANES
    sizes = (heads, page, pages, rows, steps, pages_max, requests)
    dest = page_dest.reshape(1, pages)
    slot_width = 32
    f32, bf16, i32 = jnp.float32, jnp.bfloat16, jnp.int32
    shape = jax.ShapeDtypeStruct

    direct = instances <= DIRECT and instances & (instances - 1) == 0
    queries = query_rows(dec_q[0])
    if direct:
        arrived = {x: swap(queries, x, instances) for x in range(1, instances)}

    fresh = dec_new.reshape(-1, LANES)
    source_kv = prefill_kv.reshape(-1, LANES)
    cache = cache_kv.reshape(-1, LANES)
    lengths = jnp.broadcast_to(span_len[:, None], (1, pages))
    ints = (page_seg, dest, page_row, lengths, block_table, cache_len)
    info, *state, keys, vals, own_q = pl.pallas_call(
        functools.partial(cache_kernel, sizes),
        out_shape=(
            shape((8, slot_width), i32),
            *[shape((rows * per_row, LANES), f32)] * 3,
            shape((span, heads * LANES), bf16),
            shape((span, heads * LANES), bf16),
            shape(queries.shape, bf16),
        ),
        in_specs=[HBM_SPEC] * 10,
        out_specs=(SMEM_SPEC,) + (VMEM_SPEC,) * 6,
        scratch_shapes=[pltpu.SMEM(x.shape, i32) for x in ints]
        + [
            pltpu.VMEM((-(-fresh.shape[0] // LANES) * LANES, LANES), bf16),
            pltpu.VMEM(cache.shape, bf16),
            pltpu.VMEM(source_kv.shape, bf16),
            pltpu.VMEM((span * heads, LANES), f32),
            pltpu.SemaphoreType.DMA((10,)),
        ],
        compiler_params=params(),
        cost_estimate=BRIEF,
        name="cache",
    )(*map(in_hbm, (*ints, queries, fresh, cache, source_kv)))
    count = requests * per_row
    tall = count + -(-(3 * -(-count // LANES) + 2) // 16) * 16
    token = shape((8, LANES), f32)

    def attend_pages(partners, slots, after):
        return pl.pallas_call(
            functools.partial(
                pages_kernel,
                (heads, page, pages, rows, requests, capacity, instances),
                partners,
            ),
            out_shape=(shape((count, LANES), f32), shape((tall, LANES), bf16), token),
            in_specs=[SMEM_SPEC] + [VMEM_SPEC] * (len(slots) + 2) + [ANY_SPEC],
            out_specs=(VMEM_SPEC,) * 3,
            scratch_shapes=[pltpu.VMEM((count, LANES), bf16)],
            compiler_params=params(),
            cost_estimate=BRIEF,
            name="pages",
        )(info, *slots, keys, vals, after)

    q_rows = query_rows(prefill_q[0])
    tile_rows = block * groups * heads
    tiles = span // block
    whole = lambda i: (0, 0)

    def attend_source(first, last, after, earlier=None):
        rest = [after] if earlier is None else [after, earlier]
        return pl.pallas_call(
            functools.partial(prefill_kernel, (heads, page, pages, block), first),
            out_shape=(shape(q_rows.shape, bf16), token),
            grid=(last - first,),
            in_specs=[SMEM_SPEC]
            + [
                pl.BlockSpec((tile_rows, LANES), lambda i: (i + first, 0)),
                pl.BlockSpec(keys.shape, whole),
                pl.BlockSpec(vals.shape, whole),
            ]
            + [ANY_SPEC] * len(rest),
            out_specs=(
                pl.BlockSpec((tile_rows, LANES), lambda i: (i + first, 0)),
                pl.BlockSpec(token.shape, whole),
            ),
            scratch_shapes=[pltpu.VMEM((page * groups * heads, block), i32)],
            input_output_aliases={} if earlier is None else {5: 0},
            compiler_params=params(),
            cost_estimate=BRIEF,
            name="prefill",
        )(info, q_rows, keys, vals, *rest)

    def join(own, sent, state, after, last):
        blocks_of = tuple(block.shape[0] // tall for block in sent)
        tag_rows = -(-2 * sum(blocks_of) // 8) * 8
        lead = [] if own is None else [own]
        whole_state = [shape((rows * per_row, LANES), f32)] * 3
        result = shape((rows * per_row, LANES), bf16)
        return pl.pallas_call(
            functools.partial(join_kernel, (rows, requests, blocks_of), own is not None, last),
            out_shape=result if last else (*whole_state, token),
            in_specs=[VMEM_SPEC] * (len(lead) + len(sent) + 3) + [ANY_SPEC],
            out_specs=VMEM_SPEC if last else (VMEM_SPEC,) * 4,
            scratch_shapes=[pltpu.VMEM(x.shape, f32) for x in whole_state if last]
            + [
                pltpu.VMEM((tag_rows, LANES), i32),
                pltpu.SMEM((tag_rows, LANES), i32),
                pltpu.SemaphoreType.DMA,
            ],
            compiler_params=params(),
            cost_estimate=BRIEF,
            name="join",
        )(*lead, *sent, *state, after)

    if direct and instances > 2:
        x, *near = range(instances - 1, 0, -1)
        own, block_own, done = attend_pages((0, x), [own_q, arrived[x]], state[0])
        far = swap(block_own, x, instances)
        prefill_out, done = attend_source(0, EARLY, done)
        _, sent, done = attend_pages(tuple(near), [arrived[x] for x in near], done)
        *state, done = join(own, [block_own, far], state, done, False)
        prefill_out, done = attend_source(EARLY, tiles, done, prefill_out)
        dec_out = join(None, [swap(sent, x, instances) for x in near[::-1]], state, done, True)
    else:
        queries = gather_all(queries)
        own, sent, done = attend_pages(None, [queries], state[0])
        prefill_out, done = attend_source(0, tiles, done)
        dec_out = join(None, [gather_all(sent)], state, done, True)

    return (
        from_rows(prefill_out, prefill_q.shape),
        from_rows(dec_out, dec_q.shape),
    )


def solution(mesh):
    return jax.shard_map(
        functools.partial(shards, mesh.shape["inst"]),
        mesh=mesh,
        in_specs=(
            P(("pool", "inst"), None, "tp", None),
            P(("pool", "inst"), None, None, "tp", None),
            P(("pool", "inst")),
            P(("pool", "inst"), None),
            P(("pool", "inst"), None, None),
            P(("pool", "inst"), None),
            P(("pool", "inst"), None, None, "tp", None),
            P(("pool", "inst"), None, None, None, "tp", None),
            P(("pool", "inst"), None, None, None, "tp", None),
            P(("pool", "inst"), None),
            P(("pool", "inst"), None),
        ),
        out_specs=(
            P(("pool", "inst"), None, "tp", None),
            P(("pool", "inst"), None, None, "tp", None),
        ),
        check_vma=False,
    )
```
